32 devices in a mesh: section: 2 (over y), dp: 4 (over z), rep: 4 (over x, core).
Axes of the slice: x: 2, y: 2, z: 4, core: 2. Of those that a mesh axis runs over, the one named last changes fastest.
Arguments:
- tokens: bfloat16 [32, 256, 768], P(('dp', 'rep')), may hold values from -6 to 6
- cotangent: bfloat16 [32, 256, 768], P(('dp', 'rep')), may hold values from -6 to 6
- pair_lengths: int32 [32, 4], P(('dp', 'rep')), may hold values from 1 to 128, 256 in all within a row
- qkv_weight: bfloat16 [2, 768, 2304], P('section', 'rep'), may hold values from -0.21875 to 0.21875
- out_weight: bfloat16 [2, 768, 768], P('section', 'rep'), may hold values from -2 to 2
- up_weight: bfloat16 [2, 768, 3072], P('section', 'rep'), may hold values from -0.21875 to 0.21875
- down_weight: bfloat16 [2, 3072, 768], P('section', 'rep'), may hold values from -0.109375 to 0.109375
- query_bias: bfloat16 [2, 768], P('section'), may hold values from -3 to 3
- value_bias: bfloat16 [2, 768], P('section'), may hold values from -3 to 3
- out_bias: bfloat16 [2, 768], P('section'), may hold values from -3 to 3
- norm1_gain: bfloat16 [2, 768], P('section'), may hold values from 0.5 to 1.5
- norm1_bias: bfloat16 [2, 768], P('section'), may hold values from -2 to 2
- up_bias: bfloat16 [2, 3072], P('section'), may hold values from -3 to 3
- down_bias: bfloat16 [2, 768], P('section'), may hold values from -3 to 3
- norm2_gain: bfloat16 [2, 768], P('section'), may hold values from 0.5 to 1.5
- norm2_bias: bfloat16 [2, 768], P('section'), may hold values from -2 to 2
Outputs:
- section_out: bfloat16 [2, 32, 256, 768], P('section', ('dp', 'rep'))
- section_in_grad: bfloat16 [2, 32, 256, 768], P('section', ('dp', 'rep'))
- qkv_weight_grad: float32 [2, 768, 2304], P('section', 'rep')
- out_weight_grad: float32 [2, 768, 768], P('section', 'rep')
- up_weight_grad: float32 [2, 768, 3072], P('section', 'rep')
- down_weight_grad: float32 [2, 3072, 768], P('section', 'rep')
- query_bias_grad: float32 [2, 768], P('section')
- value_bias_grad: float32 [2, 768], P('section')
- out_bias_grad: float32 [2, 768], P('section')
- norm1_gain_grad: float32 [2, 768], P('section')
- norm1_bias_grad: float32 [2, 768], P('section')
- up_bias_grad: float32 [2, 3072], P('section')
- down_bias_grad: float32 [2, 768], P('section')
- norm2_gain_grad: float32 [2, 768], P('section')
- norm2_bias_grad: float32 [2, 768], P('section')
The draws below stay inside these ranges and needn't reach their ends.
Inputs may be any that keep to these rules, and one draw needn't show every extreme that they name: `pair_lengths`: each row's 4 lengths sum to 256; the longest pair of every row has exactly 128 tokens.
All inputs are finite; a program needn't handle non-finite values.
Results may differ from the reference program's by a relative error of at most 0.025.
Values may be sent and summed in bfloat16 or wider, within the bound.
No kernel may reach another device: no remote copies, remote signals or barrier semaphores. Data moves between devices by JAX's collectives and lax.ppermute only.
A program may use at most 256 MiB of HBM per device.

```python
import math
import jax
import jax.numpy as jnp
import numpy as np
from jax import lax

D = 768
H = 12
FF = 3072
HD = 64
SEQ = 256
PAIRS = 4
MOST = 128
ROWS = 32


def block_levels(stream_key, extent, split, smallest, high):
    gain, own = 1.0, jax.random.fold_in(stream_key, 6)
    for axis_at, parts in split:
        steps = jnp.exp(jax.random.uniform(jax.random.fold_in(own, axis_at), (parts,), jnp.float32, smallest / len(split), high / len(split)))
        gain = gain * jnp.repeat(steps, extent[axis_at] // parts).reshape([-1 if axis == axis_at else 1 for axis in range(len(extent))])
    return gain


def profile(count, total, reach, lean):
    loads = [(1 << 20) // math.isqrt(standing ** lean) + 1 for standing in range(2, count + 1)]
    surplus, given = total - reach - (count - 1), [1] * (count - 1)
    while surplus > 0:
        candidates = [i for i in range(count - 1) if given[i] < reach]
        mass, left = sum([loads[i] for i in candidates]), surplus
        for i in candidates:
            extra = min(reach - given[i], max(1, left * loads[i] // mass), surplus)
            given[i] = given[i] + extra
            surplus = surplus - extra
    return np.array([reach] + given)


def uneven_parts(rng, number_of, total, most, slope):
    if number_of == 2:
        one = jax.random.randint(rng, (), max(1, total - most), min(most, total - 1) + 1)
        return jnp.stack([one, total - one])
    sizes = jnp.asarray(profile(number_of, total, most, slope), jnp.int32)
    couples = (number_of - 1) // 2
    source_of, sink = sizes[1:1 + 2 * couples:2], sizes[2:2 + 2 * couples:2]
    slack = jnp.minimum(source_of - 1, most - sink)
    passed = jax.random.randint(jax.random.fold_in(rng, 1), (couples,), 0, 1 << 20) % (slack + 1)
    sizes = sizes.at[1:1 + 2 * couples:2].set(source_of - passed).at[2:2 + 2 * couples:2].set(sink + passed)
    return sizes[jax.random.permutation(jax.random.fold_in(rng, 2), number_of)]


def centred(stream_key, dims, spread, reach, split=(), kind=jnp.bfloat16):
    values = spread * jax.random.normal(stream_key, dims, jnp.float32)
    if split:
        values = values * block_levels(stream_key, dims, split, -0.22, 0.18)
    return jnp.clip(values, -reach, reach).astype(kind)


def setup_inputs(seed: int = 0) -> dict:
    seeds = jax.random.split(jax.random.key(seed), 17)
    return {
        "tokens": centred(seeds[0], (ROWS, SEQ, D), 1.0, 6.0, ((0, 16),)),
        "cotangent": centred(seeds[1], (ROWS, SEQ, D), 1.0, 6.0, ((0, 16),)),
        "pair_lengths": jax.vmap(lambda own: uneven_parts(own, PAIRS, SEQ, MOST, 2))(jax.random.split(seeds[2], ROWS)).reshape((ROWS, PAIRS)).astype(jnp.int32),
        "qkv_weight": centred(seeds[3], (2, D, 3 * D), D ** -0.5, 0.21875, ((0, 2), (1, 4))),
        "out_weight": centred(seeds[4], (2, D, D), 8 ** -0.5, 2.0, ((0, 2), (1, 4))),
        "up_weight": centred(seeds[5], (2, D, FF), D ** -0.5, 0.21875, ((0, 2), (1, 4))),
        "down_weight": centred(seeds[6], (2, FF, D), FF ** -0.5, 0.109375, ((0, 2), (1, 4))),
        "query_bias": centred(seeds[7], (2, D), 0.5, 3.0, ((0, 2),)),
        "value_bias": centred(seeds[8], (2, D), 0.5, 3.0, ((0, 2),)),
        "out_bias": centred(seeds[9], (2, D), 0.5, 3.0, ((0, 2),)),
        "norm1_gain": jnp.clip(1.0 + 0.1 * jax.random.normal(seeds[10], (2, D), jnp.float32), 0.5, 1.5).astype(jnp.bfloat16),
        "norm1_bias": centred(seeds[11], (2, D), 0.3, 2.0, ((0, 2),)),
        "up_bias": centred(seeds[12], (2, FF), 0.5, 3.0, ((0, 2),)),
        "down_bias": centred(seeds[13], (2, D), 0.5, 3.0, ((0, 2),)),
        "norm2_gain": jnp.clip(1.0 + 0.1 * jax.random.normal(seeds[14], (2, D), jnp.float32), 0.5, 1.5).astype(jnp.bfloat16),
        "norm2_bias": centred(seeds[15], (2, D), 0.3, 2.0, ((0, 2),)),
    }


@jax.custom_vjp
def low(v):
    return lax.optimization_barrier(v.astype(jnp.bfloat16)).astype(jnp.float32)

@jax.custom_vjp
def low_back(v):
    return v

def low_keep(v):
    return (low(v), None)

def low_pass(kept, grad):
    return (grad,)

def back_keep(v):
    return (v, None)

def back_low(kept, grad):
    return (low(grad),)
low.defvjp(low_keep, low_pass)
low_back.defvjp(back_keep, back_low)

def rounded(value):
    return low(low_back(value))

def matmul(left_rows, right_rows):
    return jnp.dot(left_rows, right_rows, precision=lax.Precision.HIGHEST)

def layer_norm(residual, gain_row, bias_row):
    center = lax.optimization_barrier(jnp.mean(residual, axis=-1, keepdims=True))
    shifted = residual - center
    inverse = lax.rsqrt(lax.optimization_barrier(jnp.mean(shifted * shifted, axis=-1, keepdims=True)) + 1e-12)
    return shifted * inverse * gain_row + bias_row

def segment_ids(lengths):
    bounds = jnp.cumsum(lengths, axis=-1)
    places = jnp.arange(SEQ, dtype=jnp.int32)
    return lax.optimization_barrier(jnp.sum((places[None, :, None] >= bounds[:, None, :]).astype(jnp.int32), axis=-1))

def attend_row(operands):
    queries, key_rows, values, segment = operands
    scores = jnp.einsum('qhe,khe->hqk', queries.reshape(SEQ, H, HD), key_rows.reshape(SEQ, H, HD), precision=lax.Precision.HIGHEST) * HD ** (-0.5)
    scores = low_back(scores)
    same_pair = segment[:, None] == segment[None, :]
    scores = jnp.where(same_pair[None], scores, -1e+30)
    highest = lax.optimization_barrier(jnp.max(scores, axis=-1, keepdims=True))
    raised = jnp.exp(scores - highest)
    weights = raised / lax.optimization_barrier(jnp.sum(raised, axis=-1, keepdims=True))
    mixed_heads = jnp.einsum('hqk,khe->qhe', low(weights), values.reshape(SEQ, H, HD), precision=lax.Precision.HIGHEST)
    return mixed_heads.reshape(SEQ, D)

def layer(inputs, segment, params):
    qkv_matrix, out_matrix, up_matrix, down_matrix, query_shift, value_shift, out_shift, gain_one, bias_one, up_shift, down_shift, gain_two, bias_two = params
    rows_count = inputs.shape[0]
    flat_rows = inputs.reshape(-1, D)
    projected = matmul(flat_rows, qkv_matrix)
    queries = rounded(projected[:, :D] + query_shift)
    key_rows = rounded(projected[:, D:2 * D])
    values = rounded(projected[:, 2 * D:] + value_shift)
    mixed_heads = lax.map(jax.checkpoint(attend_row), (queries.reshape(rows_count, SEQ, D), key_rows.reshape(rows_count, SEQ, D), values.reshape(rows_count, SEQ, D), segment))
    mixed_heads = rounded(mixed_heads.reshape(-1, D))
    attention = low_back(matmul(mixed_heads, out_matrix) + out_shift)
    hidden = layer_norm(flat_rows + attention, gain_one, bias_one)
    before_act = low_back(matmul(low(hidden), up_matrix) + up_shift)
    activation = low(jax.nn.gelu(before_act, approximate=False))
    branch = low_back(matmul(activation, down_matrix) + down_shift)
    result = layer_norm(hidden + branch, gain_two, bias_two)
    return result.reshape(inputs.shape)

def forward(params, shift_in, inputs, segment):
    first_params = tuple((stacked[0] for stacked in params))
    second_params = tuple((stacked[1] for stacked in params))
    first_out = low_back(low(layer(inputs, segment, first_params)))
    final_out = low(layer(first_out + shift_in, segment, second_params))
    return (final_out, first_out)

def reference(tokens, cotangent, pair_lengths, qkv_weight, out_weight, up_weight, down_weight, query_bias, value_bias, out_bias, norm1_gain, norm1_bias, up_bias, down_bias, norm2_gain, norm2_bias):
    params = tuple((weight.astype(jnp.float32) for weight in (qkv_weight, out_weight, up_weight, down_weight, query_bias, value_bias, out_bias, norm1_gain, norm1_bias, up_bias, down_bias, norm2_gain, norm2_bias)))
    groups = ROWS // 8
    segments = segment_ids(pair_lengths).reshape(groups, 8, SEQ)
    token_groups = tokens.astype(jnp.float32).reshape(groups, 8, SEQ, D)
    cot_groups = cotangent.astype(jnp.float32).reshape(groups, 8, SEQ, D)

    def group_step(running, operands):
        token_group, cot_group, segment = operands
        zero_shift = jnp.zeros_like(token_group)

        def local_forward(stacked, shift_in, inputs):
            return forward(stacked, shift_in, inputs, segment)
        final_out, pull_back, first_out = jax.vjp(local_forward, params, zero_shift, token_group, has_aux=True)
        param_grads, shift_grad, token_grad = pull_back(cot_group)
        running = jax.tree.map(jnp.add, running, param_grads)
        return (running, (first_out.astype(jnp.bfloat16), final_out.astype(jnp.bfloat16), token_grad.astype(jnp.bfloat16), shift_grad.astype(jnp.bfloat16)))
    initial = jax.tree.map(jnp.zeros_like, params)
    gradients, produced = lax.scan(group_step, initial, (token_groups, cot_groups, segments))
    first_outs, final_outs, token_grads, shift_grads = produced
    section_out = jnp.stack([first_outs.reshape(ROWS, SEQ, D), final_outs.reshape(ROWS, SEQ, D)])
    section_in_grad = jnp.stack([token_grads.reshape(ROWS, SEQ, D), shift_grads.reshape(ROWS, SEQ, D)])
    return (section_out, section_in_grad, gradients[0], gradients[1], gradients[2], gradients[3], gradients[4], gradients[5], gradients[6], gradients[7], gradients[8], gradients[9], gradients[10], gradients[11], gradients[12])
```

```python
from types import SimpleNamespace

import jax
import jax.numpy as jnp
from jax import lax
from jax.experimental import pallas as pl
from jax.experimental.pallas import tpu as pltpu
from jax.sharding import PartitionSpec as P

D = 768
H = 12
FF = 3072
HD = 64
SEQ = 256
SLAB = 128
WIDE = 768
HIGH = jnp.float32
LOW = jnp.bfloat16
VMEM_LIMIT = 56 << 20
PER_MICRO = 1_150_000_000


def mm(left, right):
    return lax.dot_general(left, right, (((1,), (0,)), ((), ())), preferred_element_type=HIGH)


def mm_nt(left, right):
    return lax.dot_general(left, right, (((1,), (1,)), ((), ())), preferred_element_type=HIGH)


def mm_tn(left, right):
    return lax.dot_general(left, right, (((0,), (0,)), ((), ())), preferred_element_type=HIGH)


def columns(step, width=WIDE):
    return pl.ds(pl.multiple_of(step * width, width), width)


def normalize(residual):
    center = jnp.mean(residual, axis=-1, keepdims=True)
    shifted = residual - center
    inverse = lax.rsqrt(jnp.mean(shifted * shifted, axis=-1, keepdims=True) + 1e-12)
    return shifted * inverse, inverse


def norm_back(gradient, normed, inverse, gain_row):
    scaled = gradient * gain_row
    return inverse * (
        scaled
        - jnp.mean(scaled, axis=-1, keepdims=True)
        - normed * jnp.mean(scaled * normed, axis=-1, keepdims=True)
    )


def gelu_parts(u):
    size = jnp.abs(u) * 0.7071067811865476
    t = 1.0 / (1.0 + 0.3275911 * size)
    tail = t * (
        0.127414796 + t * (-0.142248368 + t * (0.7107068705 + t * (-0.7265760135 + t * 0.5307027145)))
    )
    bell = jnp.exp(u * u * -0.5)
    tail = tail * bell
    return jnp.where(u < 0.0, tail, 1.0 - tail), bell


def column_sum(value):
    return jnp.sum(value.astype(HIGH), axis=0, keepdims=True)


def vector(ref):
    return ref[...].astype(HIGH)


FULL = dict(qkv=(D, 3 * D), out=(D, D), up=(D, FF), down=(FF, D))
STATE = dict(
    x=((SEQ, D), LOW),
    qkv=((SEQ, 3 * D), LOW),
    probs=((H, SEQ, SEQ), LOW),
    mixed=((SEQ, D), LOW),
    normed1=((SEQ, D), HIGH),
    inverse1=((SEQ, 1), HIGH),
    low=((SEQ, D), LOW),
    slope=((SEQ, FF), LOW),
    act=((SEQ, FF), LOW),
    normed2=((SEQ, D), HIGH),
    inverse2=((SEQ, 1), HIGH),
)
SUMS = dict(
    gain2=D, bias2=D, down_bias=D, up_bias=FF, gain1=D, bias1=D, out_bias=D, query_bias=D, value_bias=D
)
SUM_AT = {}
for _name in SUMS:
    SUM_AT[_name] = (sum(width for _, width in SUM_AT.values()), SUMS[_name])
PIECES = 6
SUMS_WIDTH = sum(SUMS.values())
EXTRA = 16
BACK = 3


def state_of(*names):
    return {name: STATE[name] for name in names}


class Copies:
    def __init__(self, sems):
        self.sems, self.flying, self.used = sems, {}, 0

    def start(self, key, source, target):
        copy = pltpu.make_async_copy(source, target, self.sems.at[self.used])
        self.used += 1
        copy.start()
        self.flying.setdefault(id(key), []).append(copy)

    def ready(self, *keys):
        for key in keys:
            for copy in self.flying.pop(id(key), ()):
                copy.wait()

    def finish(self):
        for key in list(self.flying):
            for copy in self.flying.pop(key):
                copy.wait()

    def matrix(self, place, pieces, target):
        own, half = place[0], place[1]
        rows = target.shape[0] // 4
        short = rows // 2
        starts = []
        for near in range(2):
            starts.append((own ^ near) * rows)
            starts.append((own ^ (near + 2)) * rows + half * short)
            starts.append((own ^ (near + 2)) * rows + (1 - half) * short)
        for source, start in zip(pieces, starts):
            at = pl.ds(pl.multiple_of(start, 16), source.shape[0])
            self.start(target, source, target.at[at, :])

    def blocks(self, place, stage, parts):
        rows, column = stage.shape[0] // 4, 0
        for sent, kept in parts:
            width = sent.shape[1]
            for number in (1, 3, 0, 2):
                at = pl.ds(pl.multiple_of((place[0] ^ number) * rows, 16), rows)
                put = pl.ds(number // 2 * (sent.shape[0] // 2), rows)
                target = (kept, sent)[number % 2].at[put, :]
                self.start(target, stage.at[at, pl.ds(column, width)], target)
            column += width


class Kernel:
    def __init__(self, place):
        self.ins, self.outs, self.scratch, self.sems = [], [], [], 0
        self.matrices = []
        self.add_in(pltpu.SMEM, place=place)

    def add_in(self, space, **arrays):
        for name, value in arrays.items():
            self.ins.append((name, value, pl.BlockSpec(memory_space=space)))

    def take(self, **arrays):
        self.add_in(pltpu.VMEM, **arrays)

    def take_far(self, **arrays):
        self.add_in(pl.ANY, **arrays)

    def take_matrix(self, **matrices):
        for name, pieces in matrices.items():
            self.matrices.append(name)
            self.take_far(**{f"{name}{number}": piece for number, piece in enumerate(pieces)})
            self.hold(**{"w_" + name: (FULL[name], LOW)})
            self.sems += len(pieces)

    def add_out(self, space, shapes):
        for name, (shape, kind) in shapes.items():
            spec = pl.BlockSpec(memory_space=space)
            self.outs.append((name, jax.ShapeDtypeStruct(shape, kind), spec))

    def give(self, **shapes):
        self.add_out(pltpu.VMEM, shapes)

    def give_far(self, **shapes):
        self.add_out(pl.ANY, shapes)
        self.sems += len(shapes)

    def hold(self, **shapes):
        self.scratch += [(name, pltpu.VMEM(shape, kind)) for name, (shape, kind) in shapes.items()]

    def run(self, body, micros, sems=0):
        names = [item[0] for item in self.ins + self.outs + self.scratch]

        def kernel(*refs):
            n = SimpleNamespace(**dict(zip(names, refs[:-1])))
            copies = Copies(refs[-1])

            def load(*wanted):
                for target in wanted:
                    for name in self.matrices:
                        if getattr(n, "w_" + name) is target:
                            pieces = [getattr(n, f"{name}{number}") for number in range(PIECES)]
                            copies.matrix(n.place, pieces, target)

            n.load = load
            body(n, copies)
            copies.finish()

        outcome = pl.pallas_call(
            kernel,
            in_specs=[spec for _, _, spec in self.ins],
            out_specs=[spec for _, _, spec in self.outs],
            out_shape=[shape for _, shape, _ in self.outs],
            scratch_shapes=[item[1] for item in self.scratch]
            + [pltpu.SemaphoreType.DMA((self.sems + sems,))],
            compiler_params=pltpu.CompilerParams(vmem_limit_bytes=VMEM_LIMIT),
            cost_estimate=pl.CostEstimate(
                flops=int(micros * PER_MICRO), bytes_accessed=1 << 20, transcendentals=0
            ),
        )(*[value for _, value, _ in self.ins])
        return SimpleNamespace(**dict(zip([item[0] for item in self.outs], outcome)))


def mask_into(pair_row, pair_col, mask_ref):
    mask_ref[...] = jnp.where(pair_col[...] == pair_row[...], 0.0, -1e30)


def lane_half(rows):
    return lax.broadcasted_iota(jnp.int32, (rows, SLAB), 1) < HD


def project(x_ref, weight, query_bias, value_bias, qkv_ref):
    for part, bias in enumerate((query_bias, None, value_bias)):
        at = pl.ds(part * D, D)
        made = mm(x_ref[...], weight[:, at])
        if bias is not None:
            made = made + vector(bias)
        qkv_ref[:, at] = made.astype(LOW)


def attend(qkv_ref, mask_ref, probs_ref, mixed_ref):
    first = lane_half(SEQ)

    @pl.loop(0, H // 2, unroll=True)
    def _(slab):
        queries = qkv_ref[:, columns(slab, SLAB)] * jnp.asarray(HD ** (-0.5), LOW)
        keys = qkv_ref[:, columns(slab + D // SLAB, SLAB)]
        values_t = qkv_ref[:, columns(slab + 2 * D // SLAB, SLAB)].T
        zero = jnp.zeros_like(keys)
        mixed = []
        for half in range(2):
            own = jnp.where(first, keys, zero) if half == 0 else jnp.where(first, zero, keys)
            scores = mm_nt(own, queries) + mask_ref[...]
            raised = jnp.exp(scores - jnp.max(scores, axis=0, keepdims=True))
            probs = (raised * (1.0 / jnp.sum(raised, axis=0, keepdims=True))).astype(LOW)
            if probs_ref is not None:
                probs_ref[2 * slab + half] = probs
            mixed.append(mm(values_t[half * HD : (half + 1) * HD], probs))
        mixed_ref[:, columns(slab, SLAB)] = jnp.concatenate(mixed, axis=0).T.astype(LOW)


def attend_back(qkv_ref, probs_ref, mixed_grad_ref, grad_ref):
    first = lane_half(SEQ)

    @pl.loop(0, H // 2, unroll=True)
    def _(slab):
        queries = qkv_ref[:, columns(slab, SLAB)] * jnp.asarray(HD ** (-0.5), LOW)
        keys_t = qkv_ref[:, columns(slab + D // SLAB, SLAB)].T
        values = qkv_ref[:, columns(slab + 2 * D // SLAB, SLAB)]
        grads = mixed_grad_ref[:, columns(slab, SLAB)]
        zero = jnp.zeros_like(values)
        query_grad, key_grad, value_grad = [], [], []
        for half in range(2):
            own = jnp.where(first, values, zero) if half == 0 else jnp.where(first, zero, values)
            probs = probs_ref[2 * slab + half]
            high = probs.astype(HIGH)
            product = high * mm_nt(own, grads)
            delta = jnp.sum(product, axis=0, keepdims=True)
            score_grad = (product - high * delta).astype(LOW)
            value_grad.append(mm(probs, grads))
            key_grad.append(mm(score_grad, queries))
            query_grad.append(mm(keys_t[half * HD : (half + 1) * HD], score_grad))
        grad_ref[:, columns(slab, SLAB)] = (
            jnp.concatenate(query_grad, axis=0).T * HD ** (-0.5)
        ).astype(LOW)
        grad_ref[:, columns(slab + D // SLAB, SLAB)] = jnp.where(first, *key_grad).astype(LOW)
        grad_ref[:, columns(slab + 2 * D // SLAB, SLAB)] = jnp.where(first, *value_grad).astype(LOW)


def first_norm(n, x, mixed):
    residual = x.astype(HIGH) + (mm(mixed, n.w_out[...]) + vector(n.out_bias))
    normed, inverse = normalize(residual)
    return normed, inverse, normed * vector(n.gain1) + vector(n.bias1)


def activate(n, low, act_ref, slope_ref):
    @pl.loop(0, FF // WIDE, unroll=True)
    def _(step):
        at = columns(step)
        before = mm(low, n.w_up[:, at]) + n.up_bias[:, at].astype(HIGH)
        share, bell = gelu_parts(before)
        act_ref[:, at] = (before * share).astype(LOW)
        if slope_ref is not None:
            slope_ref[:, at] = (share + before * bell * 0.3989422804014327).astype(LOW)


def second_norm(n, hidden, act):
    return normalize(hidden + (mm(act, n.w_down[...]) + vector(n.down_bias)))


def layer_out(n, normed):
    return (normed * vector(n.gain2) + vector(n.bias2)).astype(LOW)


def feed_back(n, branch_grad, slope_ref, pre_grad_ref):
    @pl.loop(0, FF // WIDE, unroll=True)
    def _(step):
        at = columns(step)
        act_grad = mm_nt(branch_grad, n.w_down[at, :])
        pre_grad_ref[:, at] = (act_grad * slope_ref[:, at].astype(HIGH)).astype(LOW)


def start_attention(place, row, x, pair_row, pair_col, vectors, pieces):
    k = Kernel(place)
    k.take(x=x, pair_row=pair_row, pair_col=pair_col)
    k.take(query_bias=vectors.query_bias, value_bias=vectors.value_bias)
    k.take_matrix(qkv=pieces.qkv)
    k.give(mixed=((SEQ, D), LOW))
    k.hold(mask=((SEQ, SEQ), HIGH), qkv=STATE["qkv"])

    def body(n, copies):
        n.load(n.w_qkv)
        mask_into(n.pair_row.at[row], n.pair_col.at[row], n.mask)
        copies.ready(n.w_qkv)
        project(n.x.at[row], n.w_qkv, n.query_bias, n.value_bias, n.qkv)
        attend(n.qkv, n.mask, None, n.mixed)

    return k.run(body, 9).mixed


def start_middle(place, row, x, mixed, vectors, pieces):
    k = Kernel(place)
    k.take(x=x, mixed=mixed, out_bias=vectors.out_bias, gain1=vectors.gain1)
    k.take(bias1=vectors.bias1, up_bias=vectors.up_bias)
    k.take_matrix(out=pieces.out, up=pieces.up)
    k.give(hidden=((SEQ, D), HIGH), act=((SEQ, FF), LOW))

    def body(n, copies):
        n.load(n.w_out, n.w_up)
        copies.ready(n.w_out)
        _, _, hidden = first_norm(n, n.x[row], n.mixed[...])
        n.hidden[...] = hidden
        copies.ready(n.w_up)
        activate(n, hidden.astype(LOW), n.act, None)

    outcome = k.run(body, 8)
    return outcome.hidden, outcome.act


def start_last(place, hidden, act, vectors, pieces):
    k = Kernel(place)
    k.take(hidden=hidden, act=act)
    k.take(down_bias=vectors.down_bias, gain2=vectors.gain2, bias2=vectors.bias2)
    k.take_matrix(down=pieces.down)
    k.give(out=((SEQ, D), LOW))

    def body(n, copies):
        n.load(n.w_down)
        copies.ready(n.w_down)
        n.out[...] = layer_out(n, second_norm(n, n.hidden[...], n.act[...])[0])

    return k.run(body, 6).out


def there_and_back(place, row, tokens, handed, gradient, pair_row, pair_col, vectors, pieces):
    k = Kernel(place)
    k.take(tokens=tokens, handed=handed, gradient=gradient, pair_row=pair_row, pair_col=pair_col)
    k.take(**vars(vectors))
    k.take_matrix(**vars(pieces))
    k.give(out=((SEQ, D), LOW), in_grad=((SEQ, D), LOW))
    k.give_far(**{"kept_" + name: like for name, like in STATE.items()})
    k.hold(**STATE)
    k.hold(
        resid=((SEQ, D), HIGH),
        pre_grad=((SEQ, FF), LOW),
        mixed_grad=((SEQ, D), LOW),
        proj_grad=((SEQ, 3 * D), LOW),
        mask=((SEQ, SEQ), HIGH),
    )

    def body(n, copies):
        def keep(**values):
            for name, value in values.items():
                if value is not None:
                    getattr(n, name)[...] = value
                copies.start(None, getattr(n, name), getattr(n, "kept_" + name))

        n.load(n.w_qkv, n.w_out, n.w_up, n.w_down)
        keep(x=jnp.where(n.place[2] == 0, n.tokens[row], n.handed[...]))
        mask_into(n.pair_row.at[row], n.pair_col.at[row], n.mask)
        copies.ready(n.w_qkv)
        project(n.x, n.w_qkv, n.query_bias, n.value_bias, n.qkv)
        keep(qkv=None)
        attend(n.qkv, n.mask, n.probs, n.mixed)
        keep(probs=None, mixed=None)
        copies.ready(n.w_out)
        normed, inverse, hidden = first_norm(n, n.x[...], n.mixed[...])
        n.resid[...] = hidden
        keep(normed1=normed, inverse1=inverse, low=hidden.astype(LOW))
        copies.ready(n.w_up)
        activate(n, n.low[...], n.act, n.slope)
        keep(act=None, slope=None)
        copies.ready(n.w_down)
        normed, inverse = second_norm(n, n.resid[...], n.act[...])
        keep(normed2=normed, inverse2=inverse)
        n.out[...] = layer_out(n, normed)

        resid = norm_back(
            n.gradient[row].astype(HIGH), n.normed2[...], n.inverse2[...], vector(n.gain2)
        )
        n.resid[...] = resid
        feed_back(n, resid.astype(LOW), n.slope, n.pre_grad)
        hidden_grad = n.resid[...] + mm_nt(n.pre_grad[...], n.w_up[...])
        resid = norm_back(hidden_grad, n.normed1[...], n.inverse1[...], vector(n.gain1))
        n.resid[...] = resid
        n.mixed_grad[...] = mm_nt(resid.astype(LOW), n.w_out[...]).astype(LOW)
        attend_back(n.qkv, n.probs, n.mixed_grad, n.proj_grad)
        n.in_grad[...] = (n.resid[...] + mm_nt(n.proj_grad[...], n.w_qkv[...])).astype(LOW)

    outcome = k.run(body, 27)
    state = {name: getattr(outcome, "kept_" + name) for name in STATE}
    return outcome.out, outcome.in_grad, state


def take_rows(k, states, *names):
    for name in names:
        shape, kind = STATE[name]
        k.take_far(**{f"{name}_{row}": state[name] for row, state in enumerate(states)})
        k.hold(**{name: ((len(states) * shape[0], *shape[1:]), kind)})
        k.sems += len(states)


def fetch_rows(n, copies, **targets):
    for name, target in targets.items():
        length = STATE[name][0][0]
        for row in range(target.shape[0] // length):
            part = target.at[pl.ds(row * length, length)]
            copies.start(target, getattr(n, f"{name}_{row}"), part)


def give_blocks(k, name, extra, *widths):
    rows, width = FULL[name]
    k.hold(stage=((rows, width), LOW))
    for part, width in enumerate(widths):
        shape = (rows // 2 + 2 * extra * (part == 0), width)
        k.give_far(**{f"sent{part}": (shape, LOW), f"kept{part}": (shape, LOW)})
        k.sems += 2


def parts_of(outcome):
    found = vars(outcome)
    return [(found["sent" + name[4:]], found[name]) for name in found if name[:4] == "kept"]


def send_blocks(n, copies):
    copies.blocks(n.place, n.stage, parts_of(n))


def product(n, left, right):
    @pl.loop(0, n.stage.shape[1] // WIDE)
    def _(step):
        at = columns(step)
        n.stage[:, at] = mm_tn(left[...], right[:, at]).astype(LOW)


def put_sums(n, **values):
    at = 0
    for value in values.values():
        n.sums[:, at : at + value.shape[1]] = value
        at += value.shape[1]


def back_down(place, cotangent, handed, states, vectors):
    rows = len(states)
    tall = rows * SEQ
    k = Kernel(place)
    k.take(cotangent=cotangent, gain2=vectors.gain2)
    k.take(**{f"handed{row}": value for row, value in enumerate(handed)})
    take_rows(k, states, "normed2", "inverse2", "act")
    k.give(resid=((tall, D), HIGH), branch_grad=((tall, D), LOW), sums=((1, 3 * D), HIGH))
    half = FF // 8
    for part in range(2):
        k.give_far(**{f"sent{part}": ((half, 2 * D), LOW), f"kept{part}": ((half, 2 * D), LOW)})
        k.sems += 8
    k.hold(stage=((8 * half, D), LOW))

    def body(n, copies):
        fetch_rows(n, copies, normed2=n.normed2, inverse2=n.inverse2, act=n.act)
        copies.ready(n.normed2, n.inverse2)
        gradient = jnp.concatenate(
            [
                jnp.where(n.place[2] == 0, getattr(n, f"handed{row}")[...], n.cotangent[row])
                for row in range(rows)
            ],
            axis=0,
        ).astype(HIGH)
        normed = n.normed2[...]
        resid = norm_back(gradient, normed, n.inverse2[...], vector(n.gain2))
        n.resid[...] = resid
        n.branch_grad[...] = resid.astype(LOW)
        put_sums(
            n,
            gain2=column_sum(gradient * normed),
            bias2=column_sum(gradient),
            down_bias=column_sum(n.branch_grad[...]),
        )
        copies.ready(n.act)
        for part, (sent, kept) in enumerate(parts_of(n)):
            for number in (1, 3, 0, 2):
                start = (n.place[0] ^ number) * (2 * half) + part * half
                at = pl.ds(pl.multiple_of(start, half), half)
                put = (4 * part + number) * half
                n.stage[pl.ds(put, half), :] = mm_tn(n.act[:, at], n.branch_grad[...]).astype(LOW)
                target, short = (kept, sent)[number % 2], half // 2
                for side in range(2):
                    into = target.at[pl.ds(number // 2 * short, short), pl.ds(side * D, D)]
                    copies.start(target, n.stage.at[pl.ds(put + side * short, short), :], into)

    outcome = k.run(body, 9)
    return outcome, parts_of(outcome)


def back_up(place, branch_grad, states, pieces):
    tall = len(states) * SEQ
    k = Kernel(place)
    k.take(branch_grad=branch_grad)
    k.take_matrix(down=pieces.down)
    take_rows(k, states, "slope")
    k.give(pre_grad=((tall, FF), LOW), sums=((1, FF), HIGH))

    def body(n, copies):
        n.load(n.w_down)
        fetch_rows(n, copies, slope=n.slope)
        copies.ready(n.w_down, n.slope)
        feed_back(n, n.branch_grad[...], n.slope, n.pre_grad)
        put_sums(n, up_bias=column_sum(n.pre_grad[...]))

    return k.run(body, 9)


def up_product(place, pre_grad, states):
    k = Kernel(place)
    k.take(pre_grad=pre_grad)
    take_rows(k, states, "low")
    give_blocks(k, "up", 0, FF)

    def body(n, copies):
        fetch_rows(n, copies, low=n.low)
        copies.ready(n.low)
        product(n, n.low, n.pre_grad)
        send_blocks(n, copies)

    return parts_of(k.run(body, 6))


def back_hidden(place, resid, pre_grad, states, vectors, pieces):
    tall = len(states) * SEQ
    k = Kernel(place)
    k.take(old_resid=resid, pre_grad=pre_grad, gain1=vectors.gain1)
    k.take_matrix(up=pieces.up)
    take_rows(k, states, "normed1", "inverse1", "mixed")
    k.give(resid=((tall, D), HIGH), mixer_grad=((tall, D), LOW), sums=((1, 3 * D), HIGH))
    give_blocks(k, "out", 0, D)

    def body(n, copies):
        n.load(n.w_up)
        fetch_rows(n, copies, normed1=n.normed1, inverse1=n.inverse1, mixed=n.mixed)
        copies.ready(n.w_up, n.normed1, n.inverse1)
        hidden_grad = n.old_resid[...] + mm_nt(n.pre_grad[...], n.w_up[...])
        normed = n.normed1[...]
        resid = norm_back(hidden_grad, normed, n.inverse1[...], vector(n.gain1))
        n.resid[...] = resid
        n.mixer_grad[...] = resid.astype(LOW)
        put_sums(
            n,
            gain1=column_sum(hidden_grad * normed),
            bias1=column_sum(hidden_grad),
            out_bias=column_sum(n.mixer_grad[...]),
        )
        copies.ready(n.mixed)
        product(n, n.mixed, n.mixer_grad)
        send_blocks(n, copies)

    outcome = k.run(body, 2)
    return outcome, parts_of(outcome)


def back_mix(place, row, mixer_grad, states, pieces, first=None, sums=None):
    k = Kernel(place)
    k.take_far(all_grad=mixer_grad)
    k.take_matrix(out=pieces.out)
    take_rows(k, states[row : row + 1], "qkv", "probs")
    k.hold(mixer_grad=((SEQ, D), LOW), mixed_grad=((SEQ, D), LOW))
    k.give(proj_grad=((SEQ, 3 * D), LOW), sums=((1, 2 * D), HIGH))
    if first is not None:
        k.take(first_sums=first.sums, sums0=sums[0], sums1=sums[1], sums2=sums[2])
        k.take_far(first_grad=first.proj_grad)
        k.hold(proj0=((SEQ, 3 * D), LOW), all_sums=((1, SUMS_WIDTH), HIGH))
        k.hold(sums_stage=((4 * EXTRA, 3 * D), LOW))
        take_rows(k, states, "x")
        give_blocks(k, "qkv", EXTRA, 3 * D)
        k.sems += 4

    def body(n, copies):
        copies.start(n.mixer_grad, n.all_grad.at[pl.ds(row * SEQ, SEQ), :], n.mixer_grad)
        n.load(n.w_out)
        fetch_rows(n, copies, qkv=n.qkv, probs=n.probs)
        if first is not None:
            fetch_rows(n, copies, x=n.x)
            copies.start(n.proj0, n.first_grad, n.proj0)
        copies.ready(n.mixer_grad, n.w_out)
        n.mixed_grad[...] = mm_nt(n.mixer_grad[...], n.w_out[...]).astype(LOW)
        copies.ready(n.qkv, n.probs)
        attend_back(n.qkv, n.probs, n.mixed_grad, n.proj_grad)
        sums = dict(
            query_bias=column_sum(n.proj_grad[:, :D]),
            value_bias=column_sum(n.proj_grad[:, 2 * D :]),
        )
        put_sums(n, **sums)
        if first is not None:
            at = 0
            for part in (n.sums0[...], n.sums1[...], n.sums2[...], n.sums[...] + n.first_sums[...]):
                n.all_sums[:, at : at + part.shape[1]] = part
                at += part.shape[1]
            quarter = SUMS_WIDTH // 4
            n.sums_stage[...] = jnp.zeros_like(n.sums_stage)
            for number in (1, 3, 0, 2):
                start = (n.place[0] ^ number) * quarter
                own = n.all_sums[:, pl.ds(pl.multiple_of(start, SLAB), quarter)].astype(LOW)
                base = number * EXTRA
                for line in range(3):
                    at = slice(line * D, (line + 1) * D)
                    n.sums_stage[base + line : base + line + 1, D : 2 * D] = own[:, at]
                target = (n.kept0, n.sent0)[number % 2]
                block = target.shape[0] // 2
                put = pl.ds((number // 2 + 1) * block - EXTRA, EXTRA)
                copies.start(target, n.sums_stage.at[pl.ds(base, EXTRA), :], target.at[put, :])
            copies.ready(n.x, n.proj0)

            @pl.loop(0, 3)
            def _(step):
                at = columns(step)
                n.stage[:, at] = (
                    mm_tn(n.x[:SEQ], n.proj0[:, at]) + mm_tn(n.x[SEQ:], n.proj_grad[:, at])
                ).astype(LOW)

            send_blocks(n, copies)

    return k.run(body, 10 if first is None else 14, 3)


def back_input(place, resid, first, second, pieces):
    k = Kernel(place)
    k.take(resid=resid, first=first, second=second)
    k.take_matrix(qkv=pieces.qkv)
    k.give(in_grad=((2, SEQ, D), LOW))

    def body(n, copies):
        n.load(n.w_qkv)
        copies.ready(n.w_qkv)
        for row, grad in enumerate((n.first, n.second)):
            total = n.resid[pl.ds(row * SEQ, SEQ), :] + mm_nt(grad[...], n.w_qkv[...])
            n.in_grad[row] = total.astype(LOW)

    return k.run(body, 5).in_grad


def swap(value, axis, bit):
    devices = lax.axis_size(axis)
    return lax.ppermute(value, axis, [(i, i ^ bit) for i in range(devices)])


def half_of(shard):
    rows = shard.shape[0] // 2
    return lax.dynamic_slice_in_dim(shard, lax.axis_index("dp") % 2 * rows, rows, axis=0)


def all_pieces(shard, far, other):
    return [shard, far, other, swap(shard, "rep", 1), swap(far, "rep", 1), swap(other, "rep", 1)]


def add_low(*values):
    total = values[0].astype(HIGH)
    for value in values[1:]:
        total = total + value.astype(HIGH)
    return total.astype(LOW)


def after(value, *others):
    others = [other for other in others if other is not None]
    return lax.optimization_barrier((value, *others))[0] if others else value


def fit(value, shape):
    return jnp.pad(value, [(0, want - have) for want, have in zip(shape, value.shape)])


def common(first, second):
    return tuple(max(pair) for pair in zip(first.shape, second.shape))


def part_of(value, rows, columns):
    return value[rows[0] : rows[1], columns[0] : columns[1]]


class Reduction:
    def __init__(self):
        self.x, self.ends, self.across = [], [], []
        self.sums, self.totals, self.finals = [], [], []
        index = lax.axis_index("dp")
        self.line = lax.axis_size("dp") == 4
        self.edge = (index == 0) | (index == 3)

    def push(self, own, far):
        self.x.append(swap(after(far, *self.x[-1:]), "rep", 2))
        total = add_low(*own, self.x[-1])
        if self.line:
            self.turn(total)
        else:
            self.finals.append(lax.psum(total, "dp").astype(HIGH))

    def turn(self, total):
        at = len(self.ends)
        back = self.totals[at - BACK] if at >= BACK else None
        if total is None or back is None:
            payload = back if total is None else total
        else:
            shape = common(total, back)
            payload = jnp.where(self.edge, fit(total, shape), fit(back, shape))
        arrived = swap(after(payload, *self.ends[-1:]), "dp", 1)
        self.ends.append(arrived)
        if back is not None:
            here = arrived[: back.shape[0], : back.shape[1]]
            self.finals.append(jnp.where(self.edge, here, back).astype(HIGH))
        if total is not None:
            sums = add_low(total, arrived[: total.shape[0], : total.shape[1]])
            self.across.append(
                lax.ppermute(sums, "dp", [(1, 2), (2, 1)])
            )
            self.totals.append(add_low(sums, self.across[-1]))

    def finish(self):
        if self.line:
            for _ in range(BACK):
                self.turn(None)
        return self.finals


def between_cores(parts):
    own, far = [], []
    for sent, kept in parts:
        rows = kept.shape[0] // 2
        arrived = swap(sent, "rep", 1)
        own.append((kept[:rows], arrived[:rows]))
        far.append((kept[rows:], arrived[rows:]))
    return own, far


def spread(value):
    index = lax.axis_index("rep")
    for bit in (1, 2):
        other = swap(value, "rep", bit)
        high = (index & bit) > 0
        value = jnp.concatenate([jnp.where(high, other, value), jnp.where(high, value, other)])
    return value


def segment_ids(lengths):
    bounds = jnp.cumsum(lengths, axis=-1)
    places = jnp.arange(SEQ, dtype=jnp.int32)
    return jnp.sum((places[None, :, None] >= bounds[:, None, :]).astype(jnp.int32), axis=-1)


def per_device(
    tokens,
    cotangent,
    pair_lengths,
    qkv_weight,
    out_weight,
    up_weight,
    down_weight,
    query_bias,
    value_bias,
    out_bias,
    norm1_gain,
    norm1_bias,
    up_bias,
    down_bias,
    norm2_gain,
    norm2_bias,
):
    rows = tokens.shape[0]
    place = jnp.stack(
        [lax.axis_index("rep"), lax.axis_index("dp") % 2, lax.axis_index("section")]
    ).astype(jnp.int32)
    vectors = SimpleNamespace(
        query_bias=query_bias,
        value_bias=value_bias,
        out_bias=out_bias,
        gain1=norm1_gain,
        bias1=norm1_bias,
        up_bias=up_bias,
        down_bias=down_bias,
        gain2=norm2_gain,
        bias2=norm2_bias,
    )
    pairs = segment_ids(pair_lengths)
    pair_row, pair_col = pairs[:, None, :], pairs[:, :, None]

    shards = SimpleNamespace(
        qkv=qkv_weight[0], out=out_weight[0], up=up_weight[0], down=down_weight[0]
    )
    far, other, pieces = SimpleNamespace(), SimpleNamespace(), SimpleNamespace()
    far.qkv = swap(half_of(shards.qkv), "rep", 2)
    far.out = swap(half_of(shards.out), "rep", 2)
    far.up = swap(after(half_of(shards.up), far.qkv, far.out), "rep", 2)
    other.qkv = swap(after(far.qkv, far.out), "dp", 1)
    other.out = swap(after(far.out, far.qkv), "dp", 1)
    pieces.out = all_pieces(shards.out, far.out, other.out)
    pieces.qkv = all_pieces(shards.qkv, far.qkv, other.qkv)
    mixed = [start_attention(after(place, other.out, far.up), 0, tokens, pair_row, pair_col, vectors, pieces)]
    other.up = swap(after(far.up, other.qkv, other.out), "dp", 1)
    far.down = swap(after(half_of(shards.down), far.up, other.qkv), "rep", 2)
    pieces.up = all_pieces(shards.up, far.up, other.up)
    mixed.append(
        start_attention(
            after(place, mixed[0], other.up, far.down), 1, tokens, pair_row, pair_col, vectors, pieces
        )
    )
    other.down = swap(after(far.down, other.up), "dp", 1)
    pieces.down = all_pieces(shards.down, far.down, other.down)
    handed = []
    middle = []
    for row in range(rows):
        middle.append(
            start_middle(after(place, *(other.down, mixed[1])[1 - row :]), row, tokens, mixed[row], vectors, pieces)
        )
    for row in range(rows):
        out = start_last(place, *middle[row], vectors, pieces)
        handed.append(lax.ppermute(out, "section", [(0, 1)]))

    outs, states, handed_back = [], [], []
    for row in range(rows):
        out, in_grad, state = there_and_back(
            place, row, tokens, handed[row], cotangent, pair_row, pair_col, vectors, pieces
        )
        outs.append(out)
        states.append(state)
        handed_back.append(lax.ppermute(in_grad, "section", [(1, 0)]))

    reduction = Reduction()
    fed, down_parts = back_down(place, cotangent, handed_back, states, vectors)
    own, far = between_cores(down_parts)
    fars = [add_low(*item) for item in far]
    raised = back_up(after(place, fars[0]), fed.branch_grad, states, pieces)
    reduction.push(own[0], fars[0])
    reduction.push(own[1], fars[1])
    up_parts = up_product(place, raised.pre_grad, states)
    own, far = between_cores(up_parts)
    for step in range(2):
        at = slice(step * FF // 2, (step + 1) * FF // 2)
        reduction.push([value[:, at] for value in own[0]], add_low(*[v[:, at] for v in far[0]]))
    hid, out_parts = back_hidden(
        after(place, up_parts[0][0], reduction.x[0]),
        fed.resid,
        raised.pre_grad,
        states,
        vectors,
        pieces,
    )
    out_own, out_far = between_cores(out_parts)
    first = back_mix(after(place, reduction.x[1]), 0, hid.mixer_grad, states, pieces)
    sums = (fed.sums, raised.sums, hid.sums)
    second = back_mix(place, 1, hid.mixer_grad, states, pieces, first, sums)
    own, far = between_cores(parts_of(second))

    def beside(left, right):
        return [jnp.concatenate([a, b[: D // 4, :D]], axis=1) for a, b in zip(left, right)]

    reduction.push(beside(out_own[0], own[0]), add_low(*beside(out_far[0], far[0])))
    reduction.push([v[:, D : 2 * D] for v in own[0]], add_low(*[v[:, D : 2 * D] for v in far[0]]))
    tail = [[v[: D // 4, 2 * D :] for v in values] for values in (own[0], far[0])]
    reduction.push(tail[0], add_low(*tail[1]))
    in_grads = back_input(
        after(place, reduction.x[2]), hid.resid, first.proj_grad, second.proj_grad, pieces
    )
    down0, down1, up0, up1, mix, qkv1, qkv2 = reduction.finish()
    block = qkv1[D // 4 :]
    sums = spread(block[:3].reshape(3 * D).astype(LOW))[None].astype(HIGH)
    totals = [
        jnp.concatenate([mix[:, D:], qkv1[: D // 4], qkv2], axis=1),
        mix[:, :D],
        jnp.concatenate([up0, up1], axis=1),
        jnp.concatenate([down0[:, :D], down0[:, D:], down1[:, :D], down1[:, D:]], axis=0),
    ]
    vector_totals = [
        sums[:, SUM_AT[name][0] : SUM_AT[name][0] + SUM_AT[name][1]] for name in vars(vectors)
    ]
    return (
        jnp.stack(outs)[None],
        in_grads[None],
        *[total[None] for total in totals],
        *vector_totals,
    )


def solution(mesh):
    rows = P(("dp", "rep"), None, None)
    matrix = P("section", "rep", None)
    row = P("section", None)
    made = P("section", ("dp", "rep"), None, None)
    return jax.shard_map(
        per_device,
        mesh=mesh,
        in_specs=(rows, rows, P(("dp", "rep"), None)) + (matrix,) * 4 + (row,) * 9,
        out_specs=(made, made) + (matrix,) * 4 + (row,) * 9,
        check_vma=False,
    )
```

```python
from types import SimpleNamespace

import jax
import jax.numpy as jnp
from jax import lax
from jax.experimental import pallas as pl
from jax.experimental.pallas import tpu as pltpu
from jax.sharding import PartitionSpec as P

D = 768
H = 12
FF = 3072
HD = 64
SEQ = 256
SLAB = 128
WIDE = 768
HIGH = jnp.float32
LOW = jnp.bfloat16
VMEM_LIMIT = 56 << 20
PER_MICRO = 1_150_000_000


def mm(left, right):
    return lax.dot_general(left, right, (((1,), (0,)), ((), ())), preferred_element_type=HIGH)


def mm_nt(left, right):
    return lax.dot_general(left, right, (((1,), (1,)), ((), ())), preferred_element_type=HIGH)


def mm_tn(left, right):
    return lax.dot_general(left, right, (((0,), (0,)), ((), ())), preferred_element_type=HIGH)


def columns(step, width=WIDE):
    return pl.ds(pl.multiple_of(step * width, width), width)


def normalize(residual):
    center = jnp.mean(residual, axis=-1, keepdims=True)
    shifted = residual - center
    inverse = lax.rsqrt(jnp.mean(shifted * shifted, axis=-1, keepdims=True) + 1e-12)
    return shifted * inverse, inverse


def norm_back(gradient, normed, inverse, gain_row):
    scaled = gradient * gain_row
    return inverse * (
        scaled
        - jnp.mean(scaled, axis=-1, keepdims=True)
        - normed * jnp.mean(scaled * normed, axis=-1, keepdims=True)
    )


def gelu_parts(u):
    t = 1.0 / (1.0 + 0.23164188 * jnp.abs(u))
    tail = t * (
        0.127414796 + t * (-0.142248368 + t * (0.7107068705 + t * (-0.7265760135 + t * 0.5307027145)))
    )
    bell = jnp.exp(u * u * -0.5)
    tail = tail * bell
    return jnp.where(u < 0.0, tail, 1.0 - tail), bell


def column_sum(value):
    return jnp.sum(value.astype(HIGH), axis=0, keepdims=True)


def vector(ref):
    return ref[...].astype(HIGH)


FULL = dict(qkv=(D, 3 * D), out=(D, D), up=(D, FF), down=(FF, D))
STATE = dict(
    x=((SEQ, D), LOW),
    qkv=((SEQ, 3 * D), LOW),
    probs=((H, SEQ, SEQ), LOW),
    mixed=((SEQ, D), LOW),
    normed1=((SEQ, D), HIGH),
    inverse1=((SEQ, 1), HIGH),
    low=((SEQ, D), LOW),
    slope=((SEQ, FF), LOW),
    act=((SEQ, FF), LOW),
    normed2=((SEQ, D), HIGH),
    inverse2=((SEQ, 1), HIGH),
)
SUMS = dict(
    gain2=D, bias2=D, down_bias=D, up_bias=FF, gain1=D, bias1=D, out_bias=D, query_bias=D, value_bias=D
)
SUM_AT = {}
for _name in SUMS:
    SUM_AT[_name] = (sum(width for _, width in SUM_AT.values()), SUMS[_name])
PIECES = 6
COLUMN = dict(out=0, up=D)
SUMS_WIDTH = sum(SUMS.values())
EXTRA = 16
BACK = 2


def state_of(*names):
    return {name: STATE[name] for name in names}


class Copies:
    def __init__(self, sems):
        self.sems, self.flying, self.used = sems, {}, 0

    def start(self, key, source, target):
        copy = pltpu.make_async_copy(source, target, self.sems.at[self.used])
        self.used += 1
        copy.start()
        self.flying.setdefault(id(key), []).append(copy)

    def ready(self, *keys):
        for key in keys:
            for copy in self.flying.pop(id(key), ()):
                copy.wait()

    def finish(self):
        for key in list(self.flying):
            for copy in self.flying.pop(key):
                copy.wait()

    def matrix(self, place, pieces, target, column):
        own, half = place[0], place[1]
        rows = target.shape[0] // 4
        short = rows // 2
        starts = []
        for near in range(2):
            starts.append((own ^ near) * rows)
            starts.append((own ^ (near + 2)) * rows + half * short)
            starts.append((own ^ (near + 2)) * rows + (1 - half) * short)
        for source, start in zip(pieces, starts):
            at = pl.ds(pl.multiple_of(start, 16), source.shape[0])
            if column is not None:
                source = source.at[:, pl.ds(column, target.shape[1])]
            self.start(target, source, target.at[at, :])

    def blocks(self, place, stage, parts):
        rows, column = stage.shape[0] // 4, 0
        for sent, kept in parts:
            width = sent.shape[1]
            for number in (1, 3, 0, 2):
                at = pl.ds(pl.multiple_of((place[0] ^ number) * rows, 16), rows)
                put = pl.ds(number // 2 * (sent.shape[0] // 2), rows)
                target = (kept, sent)[number % 2].at[put, :]
                self.start(target, stage.at[at, pl.ds(column, width)], target)
            column += width


class Kernel:
    def __init__(self, place):
        self.ins, self.outs, self.scratch, self.sems = [], [], [], 0
        self.matrices = []
        self.add_in(pltpu.SMEM, place=place)

    def add_in(self, space, **arrays):
        for name, value in arrays.items():
            self.ins.append((name, value, pl.BlockSpec(memory_space=space)))

    def take(self, **arrays):
        self.add_in(pltpu.VMEM, **arrays)

    def take_far(self, **arrays):
        self.add_in(pl.ANY, **arrays)

    def take_matrix(self, **matrices):
        for name, pieces in matrices.items():
            self.matrices.append(name)
            self.take_far(**{f"{name}{number}": piece for number, piece in enumerate(pieces)})
            self.hold(**{"w_" + name: (FULL[name], LOW)})
            self.sems += len(pieces)

    def add_out(self, space, shapes):
        for name, (shape, kind) in shapes.items():
            spec = pl.BlockSpec(memory_space=space)
            self.outs.append((name, jax.ShapeDtypeStruct(shape, kind), spec))

    def give(self, **shapes):
        self.add_out(pltpu.VMEM, shapes)

    def give_far(self, **shapes):
        self.add_out(pl.ANY, shapes)
        self.sems += len(shapes)

    def hold(self, **shapes):
        self.scratch += [(name, pltpu.VMEM(shape, kind)) for name, (shape, kind) in shapes.items()]

    def pull(self, **arrays):
        for name, value in arrays.items():
            self.take_far(**{"from_" + name: value})
            self.hold(**{name: (value.shape, value.dtype)})
            self.sems += 1

    def put(self, **shapes):
        for name, like in shapes.items():
            self.give_far(**{"to_" + name: like})
            self.hold(**{name: like})

    def run(self, body, micros, sems=0):
        names = [item[0] for item in self.ins + self.outs + self.scratch]

        def kernel(*refs):
            n = SimpleNamespace(**dict(zip(names, refs[:-1])))
            copies = Copies(refs[-1])

            def load(*wanted):
                for target in wanted:
                    for name in self.matrices:
                        if getattr(n, "w_" + name) is target:
                            pieces = [getattr(n, f"{name}{number}") for number in range(PIECES)]
                            copies.matrix(n.place, pieces, target, COLUMN.get(name))

            def move(prefix, source_first):
                def start(*wanted):
                    for target in wanted:
                        for name, ref in vars(n).items():
                            if ref is target:
                                other = getattr(n, prefix + name)
                                pair = (other, target) if source_first else (target, other)
                                copies.start(target, *pair)

                return start

            n.load, n.fetch, n.send = load, move("from_", True), move("to_", False)
            body(n, copies)
            copies.finish()

        outcome = pl.pallas_call(
            kernel,
            in_specs=[spec for _, _, spec in self.ins],
            out_specs=[spec for _, _, spec in self.outs],
            out_shape=[shape for _, shape, _ in self.outs],
            scratch_shapes=[item[1] for item in self.scratch]
            + [pltpu.SemaphoreType.DMA((self.sems + sems,))],
            compiler_params=pltpu.CompilerParams(vmem_limit_bytes=VMEM_LIMIT),
            cost_estimate=pl.CostEstimate(
                flops=int(micros * PER_MICRO), bytes_accessed=1 << 20, transcendentals=0
            ),
        )(*[value for _, value, _ in self.ins])
        return SimpleNamespace(**dict(zip([item[0] for item in self.outs], outcome)))


def mask_into(pair_row, pair_col, mask_ref):
    mask_ref[...] = jnp.where(pair_col[...] == pair_row[...], 0.0, -1e30)


def lane_half(rows):
    return lax.broadcasted_iota(jnp.int32, (rows, SLAB), 1) < HD


def project(x_ref, weight, query_bias, value_bias, qkv_ref):
    for part, bias in enumerate((query_bias, None, value_bias)):
        at = pl.ds(part * D, D)
        made = mm(x_ref[...], weight[:, at])
        if bias is not None:
            made = made + vector(bias)
        qkv_ref[:, at] = made.astype(LOW)


def attend(qkv_ref, mask_ref, probs_ref, mixed_ref):
    first = lane_half(SEQ)

    @pl.loop(0, H // 2, unroll=True)
    def _(slab):
        queries = qkv_ref[:, columns(slab, SLAB)] * jnp.asarray(HD ** (-0.5), LOW)
        keys = qkv_ref[:, columns(slab + D // SLAB, SLAB)]
        values_t = qkv_ref[:, columns(slab + 2 * D // SLAB, SLAB)].T
        zero = jnp.zeros_like(keys)
        mixed = []
        for half in range(2):
            own = jnp.where(first, keys, zero) if half == 0 else jnp.where(first, zero, keys)
            scores = mm_nt(own, queries) + mask_ref[...]
            raised = jnp.exp(scores - jnp.max(scores, axis=0, keepdims=True))
            probs = (raised * (1.0 / jnp.sum(raised, axis=0, keepdims=True))).astype(LOW)
            if probs_ref is not None:
                probs_ref[2 * slab + half] = probs
            mixed.append(mm(values_t[half * HD : (half + 1) * HD], probs))
        mixed_ref[:, columns(slab, SLAB)] = jnp.concatenate(mixed, axis=0).T.astype(LOW)


def attend_back(qkv_ref, probs_ref, mixed_grad_ref, grad_ref):
    first = lane_half(SEQ)

    @pl.loop(0, H // 2, unroll=True)
    def _(slab):
        queries = qkv_ref[:, columns(slab, SLAB)] * jnp.asarray(HD ** (-0.5), LOW)
        keys_t = qkv_ref[:, columns(slab + D // SLAB, SLAB)].T
        values = qkv_ref[:, columns(slab + 2 * D // SLAB, SLAB)]
        grads = mixed_grad_ref[:, columns(slab, SLAB)]
        zero = jnp.zeros_like(values)
        query_grad, key_grad, value_grad = [], [], []
        for half in range(2):
            own = jnp.where(first, values, zero) if half == 0 else jnp.where(first, zero, values)
            probs = probs_ref[2 * slab + half]
            high = probs.astype(HIGH)
            product = high * mm_nt(own, grads)
            delta = jnp.sum(product, axis=0, keepdims=True)
            score_grad = (product - high * delta).astype(LOW)
            value_grad.append(mm(probs, grads))
            key_grad.append(mm(score_grad, queries))
            query_grad.append(mm(keys_t[half * HD : (half + 1) * HD], score_grad))
        grad_ref[:, columns(slab, SLAB)] = (
            jnp.concatenate(query_grad, axis=0).T * HD ** (-0.5)
        ).astype(LOW)
        grad_ref[:, columns(slab + D // SLAB, SLAB)] = jnp.where(first, *key_grad).astype(LOW)
        grad_ref[:, columns(slab + 2 * D // SLAB, SLAB)] = jnp.where(first, *value_grad).astype(LOW)


def first_norm(n, x, mixed):
    residual = x.astype(HIGH) + (mm(mixed, n.w_out[...]) + vector(n.out_bias))
    normed, inverse = normalize(residual)
    return normed, inverse, normed * vector(n.gain1) + vector(n.bias1)


def activate(n, low, act_ref, slope_ref):
    @pl.loop(0, FF // WIDE, unroll=True)
    def _(step):
        at = columns(step)
        before = mm(low, n.w_up[:, at]) + n.up_bias[:, at].astype(HIGH)
        share, bell = gelu_parts(before)
        act_ref[:, at] = (before * share).astype(LOW)
        if slope_ref is not None:
            slope_ref[:, at] = (share + before * bell * 0.3989422804014327).astype(LOW)


def second_norm(n, hidden, act):
    return normalize(hidden + (mm(act, n.w_down[...]) + vector(n.down_bias)))


def layer_out(n, normed):
    return (normed * vector(n.gain2) + vector(n.bias2)).astype(LOW)


def feed_back(n, branch_grad, slope_ref, pre_grad_ref):
    @pl.loop(0, FF // WIDE, unroll=True)
    def _(step):
        at = columns(step)
        act_grad = mm_nt(branch_grad, n.w_down[at, :])
        pre_grad_ref[:, at] = (act_grad * slope_ref[:, at].astype(HIGH)).astype(LOW)


def start_attention(place, x, pair_row, pair_col, vectors, pieces):
    rows = x.shape[0]
    k = Kernel(place)
    k.take(x=x, pair_row=pair_row, pair_col=pair_col)
    k.take(query_bias=vectors.query_bias, value_bias=vectors.value_bias)
    k.take_matrix(qkv=pieces.qkv)
    k.give(mixed=((rows, SEQ, D), LOW))
    k.hold(mask=((SEQ, SEQ), HIGH), qkv=STATE["qkv"])

    def body(n, copies):
        n.load(n.w_qkv)
        for row in range(rows):
            mask_into(n.pair_row.at[row], n.pair_col.at[row], n.mask)
            copies.ready(n.w_qkv)
            project(n.x.at[row], n.w_qkv, n.query_bias, n.value_bias, n.qkv)
            attend(n.qkv, n.mask, None, n.mixed.at[row])

    return k.run(body, 14).mixed


def start_middle(place, row, x, mixed, vectors, pieces):
    k = Kernel(place)
    k.take(x=x, mixed=mixed, out_bias=vectors.out_bias, gain1=vectors.gain1)
    k.take(bias1=vectors.bias1, up_bias=vectors.up_bias)
    k.take_matrix(out=pieces.out, up=pieces.up)
    k.give(hidden=((SEQ, D), HIGH), act=((SEQ, FF), LOW))

    def body(n, copies):
        n.load(n.w_out, n.w_up)
        copies.ready(n.w_out)
        _, _, hidden = first_norm(n, n.x[row], n.mixed[row])
        n.hidden[...] = hidden
        copies.ready(n.w_up)
        activate(n, hidden.astype(LOW), n.act, None)

    outcome = k.run(body, 8)
    return outcome.hidden, outcome.act


def start_last(place, hidden, act, vectors, pieces):
    k = Kernel(place)
    k.take(hidden=hidden, act=act)
    k.take(down_bias=vectors.down_bias, gain2=vectors.gain2, bias2=vectors.bias2)
    k.take_matrix(down=pieces.down)
    k.give(out=((SEQ, D), LOW))

    def body(n, copies):
        n.load(n.w_down)
        copies.ready(n.w_down)
        n.out[...] = layer_out(n, second_norm(n, n.hidden[...], n.act[...])[0])

    return k.run(body, 6).out


def start_rest(place, row, x, mixed, vectors, pieces):
    k = Kernel(place)
    k.take(x=x, mixed=mixed, out_bias=vectors.out_bias, gain1=vectors.gain1, bias1=vectors.bias1)
    k.take(up_bias=vectors.up_bias, down_bias=vectors.down_bias)
    k.take(gain2=vectors.gain2, bias2=vectors.bias2)
    k.take_matrix(out=pieces.out, up=pieces.up, down=pieces.down)
    k.give(out=((SEQ, D), LOW))
    k.hold(hidden=((SEQ, D), HIGH), act=((SEQ, FF), LOW))

    def body(n, copies):
        n.load(n.w_out, n.w_up, n.w_down)
        copies.ready(n.w_out)
        _, _, hidden = first_norm(n, n.x[row], n.mixed[row])
        n.hidden[...] = hidden
        copies.ready(n.w_up)
        activate(n, hidden.astype(LOW), n.act, None)
        copies.ready(n.w_down)
        n.out[...] = layer_out(n, second_norm(n, n.hidden[...], n.act[...])[0])

    return k.run(body, 10).out


def there_and_back(place, row, tokens, handed, gradient, pair_row, pair_col, vectors, pieces):
    k = Kernel(place)
    k.take(tokens=tokens, handed=handed, gradient=gradient, pair_row=pair_row, pair_col=pair_col)
    k.take(**vars(vectors))
    k.take_matrix(**vars(pieces))
    k.give(out=((SEQ, D), LOW), in_grad=((SEQ, D), LOW))
    k.give_far(**{"kept_" + name: like for name, like in STATE.items()})
    k.hold(**STATE)
    k.hold(
        resid=((SEQ, D), HIGH),
        pre_grad=((SEQ, FF), LOW),
        mixed_grad=((SEQ, D), LOW),
        proj_grad=((SEQ, 3 * D), LOW),
        mask=((SEQ, SEQ), HIGH),
    )

    def body(n, copies):
        def keep(**values):
            for name, value in values.items():
                if value is not None:
                    getattr(n, name)[...] = value
                copies.start(None, getattr(n, name), getattr(n, "kept_" + name))

        n.load(n.w_qkv, n.w_out, n.w_up, n.w_down)
        keep(x=jnp.where(n.place[2] == 0, n.tokens[row], n.handed[...]))
        mask_into(n.pair_row.at[row], n.pair_col.at[row], n.mask)
        copies.ready(n.w_qkv)
        project(n.x, n.w_qkv, n.query_bias, n.value_bias, n.qkv)
        keep(qkv=None)
        attend(n.qkv, n.mask, n.probs, n.mixed)
        keep(probs=None, mixed=None)
        copies.ready(n.w_out)
        normed, inverse, hidden = first_norm(n, n.x[...], n.mixed[...])
        n.resid[...] = hidden
        keep(normed1=normed, inverse1=inverse, low=hidden.astype(LOW))
        copies.ready(n.w_up)
        activate(n, n.low[...], n.act, n.slope)
        keep(act=None, slope=None)
        copies.ready(n.w_down)
        normed, inverse = second_norm(n, n.resid[...], n.act[...])
        keep(normed2=normed, inverse2=inverse)
        n.out[...] = layer_out(n, normed)

        resid = norm_back(
            n.gradient[row].astype(HIGH), n.normed2[...], n.inverse2[...], vector(n.gain2)
        )
        n.resid[...] = resid
        feed_back(n, resid.astype(LOW), n.slope, n.pre_grad)
        hidden_grad = n.resid[...] + mm_nt(n.pre_grad[...], n.w_up[...])
        resid = norm_back(hidden_grad, n.normed1[...], n.inverse1[...], vector(n.gain1))
        n.resid[...] = resid
        n.mixed_grad[...] = mm_nt(resid.astype(LOW), n.w_out[...]).astype(LOW)
        attend_back(n.qkv, n.probs, n.mixed_grad, n.proj_grad)
        n.in_grad[...] = (n.resid[...] + mm_nt(n.proj_grad[...], n.w_qkv[...])).astype(LOW)

    outcome = k.run(body, 27)
    state = {name: getattr(outcome, "kept_" + name) for name in STATE}
    return outcome.out, outcome.in_grad, state


def take_rows(k, states, *names):
    for name in names:
        shape, kind = STATE[name]
        k.take_far(**{f"{name}_{row}": state[name] for row, state in enumerate(states)})
        k.hold(**{name: ((len(states) * shape[0], *shape[1:]), kind)})
        k.sems += len(states)


def fetch_rows(n, copies, **targets):
    for name, target in targets.items():
        length = STATE[name][0][0]
        for row in range(target.shape[0] // length):
            part = target.at[pl.ds(row * length, length)]
            copies.start(target, getattr(n, f"{name}_{row}"), part)


def give_blocks(k, name, extra, *widths):
    rows, width = FULL[name]
    k.hold(stage=((rows, width), LOW))
    for part, width in enumerate(widths):
        shape = (rows // 2 + 2 * extra * (part == 0), width)
        k.give_far(**{f"sent{part}": (shape, LOW), f"kept{part}": (shape, LOW)})
        k.sems += 2


def parts_of(outcome):
    found = vars(outcome)
    return [(found["sent" + name[4:]], found[name]) for name in found if name[:4] == "kept"]


def send_blocks(n, copies):
    copies.blocks(n.place, n.stage, parts_of(n))


def product(stage, left, right):
    @pl.loop(0, stage.shape[1] // WIDE)
    def _(step):
        at = columns(step)
        stage[:, at] = mm_tn(left[...], right[:, at]).astype(LOW)


def put_sums(n, **values):
    at = 0
    for value in values.values():
        n.sums[:, at : at + value.shape[1]] = value
        at += value.shape[1]


def pull_halves(k, **arrays):
    for name, value in arrays.items():
        k.take_far(**{"first_" + name: value})
        k.hold(**{name: ((2 * SEQ, *value.shape[1:]), value.dtype)})
        k.sems += 1


def fetch_halves(n, copies, **targets):
    for name, target in targets.items():
        copies.start(target, getattr(n, "first_" + name), target.at[pl.ds(0, SEQ)])


def add_sums(sums, at, **values):
    for value in values.values():
        put = slice(at, at + value.shape[1])
        sums[:, put] = sums[:, put] + value
        at += value.shape[1]


def feed_sums(sums, at, pre_grad, hidden_grad, normed, mixer_grad):
    add_sums(
        sums,
        at,
        up_bias=column_sum(pre_grad),
        gain1=column_sum(hidden_grad * normed),
        bias1=column_sum(hidden_grad),
        out_bias=column_sum(mixer_grad),
    )


def norm_sums(sums, gradient, normed, branch_grad):
    add_sums(
        sums,
        0,
        gain2=column_sum(gradient * normed),
        bias2=column_sum(gradient),
        down_bias=column_sum(branch_grad),
    )


def projection_sums(sums, proj_grad):
    add_sums(
        sums,
        SUMS_WIDTH - 2 * D,
        query_bias=column_sum(proj_grad[:, :D]),
        value_bias=column_sum(proj_grad[:, 2 * D :]),
    )


def back_first(place, cotangent, handed, state, vectors, pieces):
    k = Kernel(place)
    k.take(cotangent=cotangent, handed=handed, gain1=vectors.gain1, gain2=vectors.gain2)
    k.take_matrix(down=pieces.down, up=pieces.up, out=pieces.out)
    names = ("normed2", "inverse2", "slope", "normed1", "inverse1", "qkv", "probs")
    k.pull(**{name: state[name] for name in names})
    k.put(
        branch_grad=((SEQ, D), LOW),
        pre_grad=((SEQ, FF), LOW),
        mixer_grad=((SEQ, D), LOW),
        proj_grad=((SEQ, 3 * D), LOW),
        resid=((SEQ, D), HIGH),
    )
    k.hold(mixed_grad=((SEQ, D), LOW))
    k.give(sums=((1, SUMS_WIDTH), HIGH))

    def body(n, copies):
        n.fetch(n.normed2, n.inverse2)
        n.load(n.w_down)
        n.fetch(n.slope)
        n.load(n.w_up)
        n.fetch(n.normed1, n.inverse1)
        n.load(n.w_out)
        n.fetch(n.qkv, n.probs)
        n.sums[...] = jnp.zeros_like(n.sums)
        copies.ready(n.normed2, n.inverse2)
        gradient = jnp.where(n.place[2] == 0, n.handed[...], n.cotangent[0]).astype(HIGH)
        normed = n.normed2[...]
        resid = norm_back(gradient, normed, n.inverse2[...], vector(n.gain2))
        n.resid[...] = resid
        n.branch_grad[...] = resid.astype(LOW)
        n.send(n.branch_grad)
        norm_sums(n.sums, gradient, normed, n.branch_grad[...])
        copies.ready(n.w_down, n.slope)
        feed_back(n, n.branch_grad[...], n.slope, n.pre_grad)
        n.send(n.pre_grad)
        copies.ready(n.w_up, n.normed1, n.inverse1)
        hidden_grad = n.resid[...] + mm_nt(n.pre_grad[...], n.w_up[...])
        normed = n.normed1[...]
        resid = norm_back(hidden_grad, normed, n.inverse1[...], vector(n.gain1))
        n.resid[...] = resid
        n.mixer_grad[...] = resid.astype(LOW)
        n.send(n.mixer_grad, n.resid)
        feed_sums(n.sums, 3 * D, n.pre_grad[...], hidden_grad, normed, n.mixer_grad[...])
        copies.ready(n.w_out, n.qkv, n.probs)
        n.mixed_grad[...] = mm_nt(n.mixer_grad[...], n.w_out[...]).astype(LOW)
        attend_back(n.qkv, n.probs, n.mixed_grad, n.proj_grad)
        n.send(n.proj_grad)
        projection_sums(n.sums, n.proj_grad)

    return k.run(body, 12)


def back_down(place, cotangent, handed, first, states, vectors):
    k = Kernel(place)
    k.take(cotangent=cotangent, handed=handed, gain2=vectors.gain2, first_sums=first.sums)
    k.pull(normed2=states[1]["normed2"], inverse2=states[1]["inverse2"])
    take_rows(k, states, "act")
    pull_halves(k, branch_grad=first.to_branch_grad)
    k.put(resid=((SEQ, D), HIGH))
    k.give_far(second_grad=((SEQ, D), LOW))
    k.give(sums=((1, SUMS_WIDTH), HIGH))
    half = FF // 8
    for part in range(2):
        k.give_far(**{f"sent{part}": ((half, 2 * D), LOW), f"kept{part}": ((half, 2 * D), LOW)})
        k.sems += 8
    k.hold(stage=((8 * half, D), LOW))

    def body(n, copies):
        n.fetch(n.normed2, n.inverse2)
        fetch_halves(n, copies, branch_grad=n.branch_grad)
        fetch_rows(n, copies, act=n.act)
        n.sums[...] = n.first_sums[...]
        copies.ready(n.normed2, n.inverse2)
        second = pl.ds(SEQ, SEQ)
        gradient = jnp.where(n.place[2] == 0, n.handed[...], n.cotangent[1]).astype(HIGH)
        normed = n.normed2[...]
        resid = norm_back(gradient, normed, n.inverse2[...], vector(n.gain2))
        n.resid[...] = resid
        n.branch_grad[second, :] = resid.astype(LOW)
        norm_sums(n.sums, gradient, normed, n.branch_grad[second, :])
        n.send(n.resid)
        copies.start(None, n.branch_grad.at[second, :], n.second_grad)
        copies.ready(n.act, n.branch_grad)
        for part, (sent, kept) in enumerate(parts_of(n)):
            for number in (1, 3, 0, 2):
                start = (n.place[0] ^ number) * (2 * half) + part * half
                at = pl.ds(pl.multiple_of(start, half), half)
                put = (4 * part + number) * half
                n.stage[pl.ds(put, half), :] = mm_tn(n.act[:, at], n.branch_grad[...]).astype(LOW)
                target, short = (kept, sent)[number % 2], half // 2
                for side in range(2):
                    into = target.at[pl.ds(number // 2 * short, short), pl.ds(side * D, D)]
                    copies.start(target, n.stage.at[pl.ds(put + side * short, short), :], into)

    outcome = k.run(body, 8)
    return outcome, parts_of(outcome)


def back_rest(place, branch_grad, resid, sums, first, states, vectors, pieces):
    second = pl.ds(SEQ, SEQ)
    k = Kernel(place)
    k.pull(branch_grad=branch_grad, old_resid=resid)
    k.take(gain1=vectors.gain1, old_sums=sums)
    k.take_matrix(down=pieces.down, up=pieces.up, out=pieces.out)
    names = ("slope", "normed1", "inverse1", "qkv", "probs")
    k.pull(**{name: states[1][name] for name in names})
    take_rows(k, states, "low", "mixed", "x")
    pull_halves(
        k,
        pre_grad=first.to_pre_grad,
        mixer_grad=first.to_mixer_grad,
        proj_grad=first.to_proj_grad,
    )
    k.hold(mixed_grad=((SEQ, D), LOW))
    k.hold(sums=((1, SUMS_WIDTH), HIGH), sums_stage=((4 * EXTRA, 3 * D), LOW))
    k.put(resid=((SEQ, D), HIGH))
    k.give_far(second_grad=((SEQ, 3 * D), LOW))
    for name, width, extra in (("up", FF, 0), ("out", D, 0), ("qkv", 3 * D, EXTRA)):
        shape = ((D // 2 + 2 * extra, width), LOW)
        k.give_far(**{"sent_" + name: shape, "kept_" + name: shape})
        k.hold(**{"stage_" + name: ((D, width), LOW)})
        k.sems += 4

    def body(n, copies):
        n.fetch(n.branch_grad)
        n.load(n.w_down)
        n.fetch(n.slope)
        fetch_halves(n, copies, pre_grad=n.pre_grad)
        fetch_rows(n, copies, low=n.low)
        n.load(n.w_up)
        n.fetch(n.old_resid, n.normed1, n.inverse1)
        n.load(n.w_out)
        fetch_halves(n, copies, mixer_grad=n.mixer_grad)
        fetch_rows(n, copies, mixed=n.mixed)
        n.fetch(n.qkv, n.probs)
        fetch_halves(n, copies, proj_grad=n.proj_grad)
        fetch_rows(n, copies, x=n.x)
        n.sums[...] = n.old_sums[...]
        copies.ready(n.branch_grad, n.w_down, n.slope)
        feed_back(n, n.branch_grad[...], n.slope, n.pre_grad.at[second, :])
        copies.ready(n.low, n.pre_grad)
        product(n.stage_up, n.low, n.pre_grad)
        copies.blocks(n.place, n.stage_up, [(n.sent_up, n.kept_up)])
        copies.ready(n.w_up, n.old_resid, n.normed1, n.inverse1)
        hidden_grad = n.old_resid[...] + mm_nt(n.pre_grad[second, :], n.w_up[...])
        normed = n.normed1[...]
        resid = norm_back(hidden_grad, normed, n.inverse1[...], vector(n.gain1))
        n.resid[...] = resid
        n.send(n.resid)
        n.mixer_grad[second, :] = resid.astype(LOW)
        feed_sums(
            n.sums, 3 * D, n.pre_grad[second, :], hidden_grad, normed, n.mixer_grad[second, :]
        )
        copies.ready(n.mixed, n.mixer_grad, n.w_out)
        product(n.stage_out, n.mixed, n.mixer_grad)
        copies.blocks(n.place, n.stage_out, [(n.sent_out, n.kept_out)])
        n.mixed_grad[...] = mm_nt(n.mixer_grad[second, :], n.w_out[...]).astype(LOW)
        copies.ready(n.qkv, n.probs)
        attend_back(n.qkv, n.probs, n.mixed_grad, n.proj_grad.at[second, :])
        copies.start(None, n.proj_grad.at[second, :], n.second_grad)
        copies.ready(n.x, n.proj_grad)
        product(n.stage_qkv, n.x, n.proj_grad)
        copies.blocks(n.place, n.stage_qkv, [(n.sent_qkv, n.kept_qkv)])
        projection_sums(n.sums, n.proj_grad[second, :])
        quarter = SUMS_WIDTH // 4
        n.sums_stage[...] = jnp.zeros_like(n.sums_stage)
        for number in (1, 3, 0, 2):
            start = (n.place[0] ^ number) * quarter
            own = n.sums[:, pl.ds(pl.multiple_of(start, SLAB), quarter)].astype(LOW)
            base = number * EXTRA
            for line in range(3):
                piece = own[:, line * D : (line + 1) * D]
                n.sums_stage[base + line : base + line + 1, :D] = piece
            target = (n.kept_qkv, n.sent_qkv)[number % 2]
            block = target.shape[0] // 2
            put = pl.ds((number // 2 + 1) * block - EXTRA, EXTRA)
            copies.start(target, n.sums_stage.at[pl.ds(base, EXTRA), :], target.at[put, :])

    return k.run(body, 22)


def back_input(place, resids, proj_grads, pieces):
    k = Kernel(place)
    k.pull(resid0=resids[0], resid1=resids[1], proj0=proj_grads[0], proj1=proj_grads[1])
    k.take_matrix(qkv=pieces.qkv)
    k.give(in_grad=((2, SEQ, D), LOW))

    def body(n, copies):
        n.fetch(n.proj0)
        n.load(n.w_qkv)
        n.fetch(n.resid0, n.proj1, n.resid1)
        copies.ready(n.w_qkv)
        for row, (resid, grad) in enumerate(((n.resid0, n.proj0), (n.resid1, n.proj1))):
            copies.ready(resid, grad)
            total = resid[...] + mm_nt(grad[...], n.w_qkv[...])
            n.in_grad[row] = total.astype(LOW)

    return k.run(body, 5).in_grad


def swap(value, axis, bit):
    devices = lax.axis_size(axis)
    return lax.ppermute(value, axis, [(i, i ^ bit) for i in range(devices)])


def half_of(shard):
    rows = shard.shape[0] // 2
    return lax.dynamic_slice_in_dim(shard, lax.axis_index("dp") % 2 * rows, rows, axis=0)


def all_pieces(shard, far, other):
    return [shard, far, other, swap(shard, "rep", 1), swap(far, "rep", 1), swap(other, "rep", 1)]


def add_low(*values):
    total = values[0].astype(HIGH)
    for value in values[1:]:
        total = total + value.astype(HIGH)
    return total.astype(LOW)


def after(value, *others):
    others = [other for other in others if other is not None]
    return lax.optimization_barrier((value, *others))[0] if others else value


def fit(value, shape):
    return jnp.pad(value, [(0, want - have) for want, have in zip(shape, value.shape)])


def common(first, second):
    return tuple(max(pair) for pair in zip(first.shape, second.shape))


def part_of(value, rows, columns):
    return value[rows[0] : rows[1], columns[0] : columns[1]]


class Reduction:
    def __init__(self):
        self.x, self.ends, self.across = [], [], []
        self.sums, self.totals, self.finals = [], [], []
        self.waiting = []
        index = lax.axis_index("dp")
        self.line = lax.axis_size("dp") == 4
        self.edge = (index == 0) | (index == 3)

    def start(self, own, far):
        self.x.append(swap(after(far, *self.x[-1:][: len(self.x) > 1]), "rep", 2))
        total = add_low(*own, self.x[-1])
        if self.line:
            self.waiting.append(total)
        else:
            self.finals.append(lax.psum(total, "dp").astype(HIGH))

    def step(self, *deps):
        if self.line:
            self.turn(after(self.waiting.pop(0), *deps))

    def turn(self, total):
        at = len(self.ends)
        back = self.totals[at - BACK] if at >= BACK else None
        if total is None or back is None:
            payload = back if total is None else total
        else:
            shape = common(total, back)
            payload = jnp.where(self.edge, fit(total, shape), fit(back, shape))
        arrived = swap(after(payload, *self.ends[-1:]), "dp", 1)
        self.ends.append(arrived)
        if back is not None:
            here = arrived[: back.shape[0], : back.shape[1]]
            self.finals.append(jnp.where(self.edge, here, back).astype(HIGH))
        if total is not None:
            sums = add_low(total, arrived[: total.shape[0], : total.shape[1]])
            self.across.append(
                lax.ppermute(sums, "dp", [(1, 2), (2, 1)])
            )
            self.totals.append(add_low(sums, self.across[-1]))

    def finish(self):
        if self.line:
            for _ in range(BACK):
                self.turn(None)
        return self.finals


def between_cores(parts):
    own, far = [], []
    for sent, kept in parts:
        rows = kept.shape[0] // 2
        arrived = swap(sent, "rep", 1)
        own.append((kept[:rows], arrived[:rows]))
        far.append((kept[rows:], arrived[rows:]))
    return own, far


def spread(value):
    index = lax.axis_index("rep")
    for bit in (1, 2):
        other = swap(value, "rep", bit)
        high = (index & bit) > 0
        value = jnp.concatenate([jnp.where(high, other, value), jnp.where(high, value, other)])
    return value


def segment_ids(lengths):
    bounds = jnp.cumsum(lengths, axis=-1)
    places = jnp.arange(SEQ, dtype=jnp.int32)
    return jnp.sum((places[None, :, None] >= bounds[:, None, :]).astype(jnp.int32), axis=-1)


def per_device(
    tokens,
    cotangent,
    pair_lengths,
    qkv_weight,
    out_weight,
    up_weight,
    down_weight,
    query_bias,
    value_bias,
    out_bias,
    norm1_gain,
    norm1_bias,
    up_bias,
    down_bias,
    norm2_gain,
    norm2_bias,
):
    rows = tokens.shape[0]
    place = jnp.stack(
        [lax.axis_index("rep"), lax.axis_index("dp") % 2, lax.axis_index("section")]
    ).astype(jnp.int32)
    vectors = SimpleNamespace(
        query_bias=query_bias,
        value_bias=value_bias,
        out_bias=out_bias,
        gain1=norm1_gain,
        bias1=norm1_bias,
        up_bias=up_bias,
        down_bias=down_bias,
        gain2=norm2_gain,
        bias2=norm2_bias,
    )
    pairs = segment_ids(pair_lengths)
    pair_row, pair_col = pairs[:, None, :], pairs[:, :, None]

    shards = SimpleNamespace(
        qkv=qkv_weight[0],
        mid=jnp.concatenate([out_weight[0], up_weight[0]], axis=1),
        down=down_weight[0],
    )
    far, other, pieces = SimpleNamespace(), SimpleNamespace(), SimpleNamespace()
    far.qkv = swap(half_of(shards.qkv), "rep", 2)
    other.qkv = swap(far.qkv, "dp", 1)
    pieces.qkv = all_pieces(shards.qkv, far.qkv, other.qkv)
    far.mid = swap(after(half_of(shards.mid), far.qkv), "rep", 2)
    mixed = start_attention(after(place, far.mid), tokens, pair_row, pair_col, vectors, pieces)
    other.mid = swap(far.mid, "dp", 1)
    far.down = swap(after(half_of(shards.down), far.mid), "rep", 2)
    pieces.up = all_pieces(shards.mid, far.mid, after(other.mid, mixed, far.down))
    pieces.out = pieces.up
    other.down = swap(after(far.down, other.mid, mixed), "dp", 1)
    hidden, act = start_middle(place, 0, tokens, mixed, vectors, pieces)
    pieces.down = all_pieces(shards.down, far.down, after(other.down, act))
    out = start_last(place, hidden, act, vectors, pieces)
    handed = [lax.ppermute(out, "section", [(0, 1)])]
    out = start_rest(after(place, out), 1, tokens, mixed, vectors, pieces)
    handed.append(lax.ppermute(out, "section", [(0, 1)]))

    outs, states, handed_back = [], [], []
    for row in range(rows):
        out, in_grad, state = there_and_back(
            place, row, tokens, handed[row], cotangent, pair_row, pair_col, vectors, pieces
        )
        outs.append(out)
        states.append(state)
        handed_back.append(lax.ppermute(in_grad, "section", [(1, 0)]))

    reduction = Reduction()
    first = back_first(place, cotangent, handed_back[0], states[0], vectors, pieces)
    fed, down_parts = back_down(place, cotangent, handed_back[1], first, states, vectors)
    own, far = between_cores(down_parts)
    fars = [add_low(*item) for item in far]
    hid = back_rest(
        after(place, fars[0], fars[1]),
        fed.second_grad,
        fed.to_resid,
        fed.sums,
        first,
        states,
        vectors,
        pieces,
    )
    reduction.start(own[0], fars[0])
    reduction.start(own[1], fars[1])
    up_own, up_far = between_cores([(hid.sent_up, hid.kept_up)])
    out_own, out_far = between_cores([(hid.sent_out, hid.kept_out)])
    own, far = between_cores([(hid.sent_qkv, hid.kept_qkv)])
    in_grads = back_input(
        after(place, *reduction.x),
        (first.to_resid, hid.to_resid),
        (first.to_proj_grad, hid.second_grad),
        pieces,
    )

    def beside(left, right):
        left = [jnp.pad(value, [(0, EXTRA), (0, 0)]) for value in left]
        return [jnp.concatenate([a, b[:, :D]], axis=1) for a, b in zip(left, right)]

    half = FF // 2
    reduction.start([v[:, :half] for v in up_own[0]], add_low(*[v[:, :half] for v in up_far[0]]))
    reduction.step(in_grads)
    reduction.start([v[:, half:] for v in up_own[0]], add_low(*[v[:, half:] for v in up_far[0]]))
    reduction.step(reduction.x[2])
    reduction.start(beside(out_own[0], own[0]), add_low(*beside(out_far[0], far[0])))
    reduction.step(reduction.x[3])
    tail = [[v[: D // 4, D:] for v in values] for values in (own[0], far[0])]
    reduction.start(tail[0], add_low(*tail[1]))
    reduction.step()
    reduction.step()
    reduction.step()
    down0, down1, up0, up1, beside, qkv = reduction.finish()
    block = beside[D // 4 :, D:]
    sums = spread(block[:3].reshape(3 * D).astype(LOW))[None].astype(HIGH)
    totals = [
        jnp.concatenate([beside[: D // 4, D:], qkv], axis=1),
        beside[: D // 4, :D],
        jnp.concatenate([up0, up1], axis=1),
        jnp.concatenate([down0[:, :D], down0[:, D:], down1[:, :D], down1[:, D:]], axis=0),
    ]
    vector_totals = [
        sums[:, SUM_AT[name][0] : SUM_AT[name][0] + SUM_AT[name][1]] for name in vars(vectors)
    ]
    return (
        jnp.stack(outs)[None],
        in_grads[None],
        *[total[None] for total in totals],
        *vector_totals,
    )


def solution(mesh):
    rows = P(("dp", "rep"), None, None)
    matrix = P("section", "rep", None)
    row = P("section", None)
    made = P("section", ("dp", "rep"), None, None)
    return jax.shard_map(
        per_device,
        mesh=mesh,
        in_specs=(rows, rows, P(("dp", "rep"), None)) + (matrix,) * 4 + (row,) * 9,
        out_specs=(made, made) + (matrix,) * 4 + (row,) * 9,
        check_vma=False,
    )
```

```python
from types import SimpleNamespace

import jax
import jax.numpy as jnp
from jax import lax
from jax.experimental import pallas as pl
from jax.experimental.pallas import tpu as pltpu
from jax.sharding import PartitionSpec as P

D = 768
H = 12
FF = 3072
HD = 64
SEQ = 256
SLAB = 128
WIDE = 768
HIGH = jnp.float32
LOW = jnp.bfloat16
VMEM_LIMIT = 56 << 20
PER_MICRO = 1_150_000_000


def mm(left, right):
    return lax.dot_general(left, right, (((1,), (0,)), ((), ())), preferred_element_type=HIGH)


def mm_nt(left, right):
    return lax.dot_general(left, right, (((1,), (1,)), ((), ())), preferred_element_type=HIGH)


def mm_tn(left, right):
    return lax.dot_general(left, right, (((0,), (0,)), ((), ())), preferred_element_type=HIGH)


def columns(step, width=WIDE):
    return pl.ds(pl.multiple_of(step * width, width), width)


def normalize(residual):
    center = jnp.mean(residual, axis=-1, keepdims=True)
    shifted = residual - center
    inverse = lax.rsqrt(jnp.mean(shifted * shifted, axis=-1, keepdims=True) + 1e-12)
    return shifted * inverse, inverse


def norm_back(gradient, normed, inverse, gain_row):
    scaled = gradient * gain_row
    return inverse * (
        scaled
        - jnp.mean(scaled, axis=-1, keepdims=True)
        - normed * jnp.mean(scaled * normed, axis=-1, keepdims=True)
    )


def gelu_parts(u):
    t = 1.0 / (1.0 + 0.23164188 * jnp.abs(u))
    tail = t * (
        0.127414796 + t * (-0.142248368 + t * (0.7107068705 + t * (-0.7265760135 + t * 0.5307027145)))
    )
    bell = jnp.exp(u * u * -0.5)
    tail = tail * bell
    return jnp.where(u < 0.0, tail, 1.0 - tail), bell


def column_sum(value):
    return jnp.sum(value.astype(HIGH), axis=0, keepdims=True)


def vector(ref):
    return ref[...].astype(HIGH)


FULL = dict(qkv=(D, 3 * D), out=(D, D), up=(D, FF), down=(FF, D))
STATE = dict(
    x=((SEQ, D), LOW),
    qkv=((SEQ, 3 * D), LOW),
    probs=((H, SEQ, SEQ), LOW),
    mixed=((SEQ, D), LOW),
    normed1=((SEQ, D), HIGH),
    inverse1=((SEQ, 1), HIGH),
    low=((SEQ, D), LOW),
    slope=((SEQ, FF), LOW),
    act=((SEQ, FF), LOW),
    normed2=((SEQ, D), HIGH),
    inverse2=((SEQ, 1), HIGH),
)
SUMS = dict(
    gain2=D, bias2=D, down_bias=D, up_bias=FF, gain1=D, bias1=D, out_bias=D, query_bias=D, value_bias=D
)
SUM_AT = {}
for _name in SUMS:
    SUM_AT[_name] = (sum(width for _, width in SUM_AT.values()), SUMS[_name])
PIECES = 6
COLUMN = dict(out=0, up=D)
SUMS_WIDTH = sum(SUMS.values())
EXTRA = 16
BACK = 2


class Copies:
    def __init__(self, sems):
        self.sems, self.flying, self.used = sems, {}, 0

    def start(self, key, source, target):
        copy = pltpu.make_async_copy(source, target, self.sems.at[self.used])
        self.used += 1
        copy.start()
        self.flying.setdefault(id(key), []).append(copy)

    def ready(self, *keys):
        for key in keys:
            for copy in self.flying.pop(id(key), ()):
                copy.wait()

    def finish(self):
        for key in list(self.flying):
            for copy in self.flying.pop(key):
                copy.wait()

    def matrix(self, place, pieces, target, column):
        own, half = place[0], place[1]
        rows = target.shape[0] // 4
        short = rows // 2
        starts = []
        for near in range(2):
            starts.append((own ^ near) * rows)
            starts.append((own ^ (near + 2)) * rows + half * short)
            starts.append((own ^ (near + 2)) * rows + (1 - half) * short)
        for source, start in zip(pieces, starts):
            at = pl.ds(pl.multiple_of(start, 16), source.shape[0])
            if column is not None:
                source = source.at[:, pl.ds(column, target.shape[1])]
            self.start(target, source, target.at[at, :])

    def blocks(self, place, stage, parts):
        rows, column = stage.shape[0] // 4, 0
        for sent, kept in parts:
            width = sent.shape[1]
            for number in (1, 3, 0, 2):
                at = pl.ds(pl.multiple_of((place[0] ^ number) * rows, 16), rows)
                put = pl.ds(number // 2 * (sent.shape[0] // 2), rows)
                target = (kept, sent)[number % 2].at[put, :]
                self.start(target, stage.at[at, pl.ds(column, width)], target)
            column += width


def back_up(place, branch_grad, resid, sums, first, states, vectors, pieces):
    second = pl.ds(SEQ, SEQ)
    k = Kernel(place)
    k.pull(branch_grad=branch_grad, old_resid=resid)
    k.take(gain1=vectors.gain1, old_sums=sums)
    k.take_matrix(down=pieces.down, up=pieces.up)
    names = ("slope", "normed1", "inverse1")
    k.pull(**{name: states[1][name] for name in names})
    take_rows(k, states, "low", "mixed")
    pull_halves(k, pre_grad=first.to_pre_grad, mixer_grad=first.to_mixer_grad)
    k.put(resid=((SEQ, D), HIGH))
    k.give_far(second_grad=((SEQ, D), LOW))
    k.give(sums=((1, SUMS_WIDTH), HIGH))
    for name, width in (("up", FF), ("out", D)):
        shape = ((D // 2, width), LOW)
        k.give_far(**{"sent_" + name: shape, "kept_" + name: shape})
        k.hold(**{"stage_" + name: ((D, width), LOW)})
        k.sems += 2

    def body(n, copies):
        n.fetch(n.branch_grad)
        n.load(n.w_down)
        n.fetch(n.slope)
        fetch_halves(n, copies, pre_grad=n.pre_grad)
        fetch_rows(n, copies, low=n.low)
        n.load(n.w_up)
        n.fetch(n.old_resid, n.normed1, n.inverse1)
        fetch_halves(n, copies, mixer_grad=n.mixer_grad)
        fetch_rows(n, copies, mixed=n.mixed)
        n.sums[...] = n.old_sums[...]
        copies.ready(n.branch_grad, n.w_down, n.slope)
        feed_back(n, n.branch_grad[...], n.slope, n.pre_grad.at[second, :])
        copies.ready(n.low, n.pre_grad)
        product(n.stage_up, n.low, n.pre_grad)
        copies.blocks(n.place, n.stage_up, [(n.sent_up, n.kept_up)])
        copies.ready(n.w_up, n.old_resid, n.normed1, n.inverse1)
        hidden_grad = n.old_resid[...] + mm_nt(n.pre_grad[second, :], n.w_up[...])
        normed = n.normed1[...]
        resid = norm_back(hidden_grad, normed, n.inverse1[...], vector(n.gain1))
        n.resid[...] = resid
        n.mixer_grad[second, :] = resid.astype(LOW)
        n.send(n.resid)
        copies.start(None, n.mixer_grad.at[second, :], n.second_grad)
        feed_sums(
            n.sums, 3 * D, n.pre_grad[second, :], hidden_grad, normed, n.mixer_grad[second, :]
        )
        copies.ready(n.mixed, n.mixer_grad)
        product(n.stage_out, n.mixed, n.mixer_grad)
        copies.blocks(n.place, n.stage_out, [(n.sent_out, n.kept_out)])

    return k.run(body, 14)


def back_mix(place, mixer_grads, resids, sums, states, pieces):
    k = Kernel(place)
    k.pull(mixer0=mixer_grads[0], mixer1=mixer_grads[1], resid0=resids[0], resid1=resids[1])
    k.take(old_sums=sums)
    k.take_matrix(out=pieces.out, qkv=pieces.qkv)
    take_rows(k, states, "qkv", "probs", "x")
    k.hold(mixed_grad=((SEQ, D), LOW), proj_grad=((2 * SEQ, 3 * D), LOW))
    k.hold(sums=((1, SUMS_WIDTH), HIGH), sums_stage=((4 * EXTRA, 3 * D), LOW))
    k.hold(stage=((D, 3 * D), LOW))
    k.give(in_grad=((2, SEQ, D), LOW))
    shape = ((D // 2 + 2 * EXTRA, 3 * D), LOW)
    k.give_far(sent0=shape, kept0=shape)
    k.sems += 8

    def body(n, copies):
        n.fetch(n.mixer0)
        n.load(n.w_out)
        fetch_rows(n, copies, qkv=n.qkv, probs=n.probs)
        n.fetch(n.mixer1)
        fetch_rows(n, copies, x=n.x)
        n.load(n.w_qkv)
        n.fetch(n.resid0, n.resid1)
        n.sums[...] = n.old_sums[...]
        copies.ready(n.w_out)
        for row, mixer_grad in enumerate((n.mixer0, n.mixer1)):
            at = pl.ds(row * SEQ, SEQ)
            copies.ready(mixer_grad)
            n.mixed_grad[...] = mm_nt(mixer_grad[...], n.w_out[...]).astype(LOW)
            copies.ready(n.qkv, n.probs)
            probs = n.probs.at[pl.ds(row * H, H)]
            attend_back(n.qkv.at[at, :], probs, n.mixed_grad, n.proj_grad.at[at, :])
        copies.ready(n.x)
        product(n.stage, n.x, n.proj_grad)
        send_blocks(n, copies)
        projection_sums(n.sums, n.proj_grad)
        quarter = SUMS_WIDTH // 4
        n.sums_stage[...] = jnp.zeros_like(n.sums_stage)
        for number in (1, 3, 0, 2):
            start = (n.place[0] ^ number) * quarter
            own = n.sums[:, pl.ds(pl.multiple_of(start, SLAB), quarter)].astype(LOW)
            base = number * EXTRA
            for line in range(3):
                piece = own[:, line * D : (line + 1) * D]
                n.sums_stage[base + line : base + line + 1, :D] = piece
            target = (n.kept0, n.sent0)[number % 2]
            block = target.shape[0] // 2
            put = pl.ds((number // 2 + 1) * block - EXTRA, EXTRA)
            copies.start(target, n.sums_stage.at[pl.ds(base, EXTRA), :], target.at[put, :])
        copies.ready(n.w_qkv)
        for row, resid in enumerate((n.resid0, n.resid1)):
            at = pl.ds(row * SEQ, SEQ)
            copies.ready(resid)
            total = resid[...] + mm_nt(n.proj_grad[at, :], n.w_qkv[...])
            n.in_grad[row] = total.astype(LOW)

    return k.run(body, 14)


class Kernel:
    def __init__(self, place):
        self.ins, self.outs, self.scratch, self.sems = [], [], [], 0
        self.matrices, self.rows = [], {}
        self.add_in(pltpu.SMEM, place=place)

    def add_in(self, space, **arrays):
        for name, value in arrays.items():
            self.ins.append((name, value, pl.BlockSpec(memory_space=space)))

    def take(self, **arrays):
        self.add_in(pltpu.VMEM, **arrays)

    def take_far(self, **arrays):
        self.add_in(pl.ANY, **arrays)

    def take_matrix(self, **matrices):
        for name, pieces in matrices.items():
            self.matrices.append(name)
            self.take_far(**{f"{name}{number}": piece for number, piece in enumerate(pieces)})
            self.hold(**{"w_" + name: (FULL[name], LOW)})
            self.sems += len(pieces)

    def add_out(self, space, shapes):
        for name, (shape, kind) in shapes.items():
            spec = pl.BlockSpec(memory_space=space)
            self.outs.append((name, jax.ShapeDtypeStruct(shape, kind), spec))

    def give(self, **shapes):
        self.add_out(pltpu.VMEM, shapes)

    def give_far(self, **shapes):
        self.add_out(pl.ANY, shapes)
        self.sems += len(shapes)

    def hold(self, **shapes):
        self.scratch += [(name, pltpu.VMEM(shape, kind)) for name, (shape, kind) in shapes.items()]

    def pull(self, **arrays):
        for name, value in arrays.items():
            self.take_far(**{"from_" + name: value})
            self.hold(**{name: (value.shape, value.dtype)})
            self.sems += 1

    def pull_row(self, row, **arrays):
        for name, value in arrays.items():
            self.take_far(**{"from_" + name: value})
            self.hold(**{name: (value.shape[1:], value.dtype)})
            self.sems += 1
            self.rows[name] = row

    def put(self, **shapes):
        for name, like in shapes.items():
            self.give_far(**{"to_" + name: like})
            self.hold(**{name: like})

    def run(self, body, micros, sems=0):
        names = [item[0] for item in self.ins + self.outs + self.scratch]

        def kernel(*refs):
            n = SimpleNamespace(**dict(zip(names, refs[:-1])))
            copies = Copies(refs[-1])

            def load(*wanted):
                for target in wanted:
                    for name in self.matrices:
                        if getattr(n, "w_" + name) is target:
                            pieces = [getattr(n, f"{name}{number}") for number in range(PIECES)]
                            copies.matrix(n.place, pieces, target, COLUMN.get(name))

            def move(prefix, source_first):
                def start(*wanted):
                    for target in wanted:
                        for name, ref in vars(n).items():
                            if ref is target:
                                other = getattr(n, prefix + name)
                                if source_first and name in self.rows:
                                    other = other.at[self.rows[name]]
                                pair = (other, target) if source_first else (target, other)
                                copies.start(target, *pair)

                return start

            n.load, n.fetch, n.send = load, move("from_", True), move("to_", False)
            body(n, copies)
            copies.finish()

        outcome = pl.pallas_call(
            kernel,
            in_specs=[spec for _, _, spec in self.ins],
            out_specs=[spec for _, _, spec in self.outs],
            out_shape=[shape for _, shape, _ in self.outs],
            scratch_shapes=[item[1] for item in self.scratch]
            + [pltpu.SemaphoreType.DMA((self.sems + sems,))],
            compiler_params=pltpu.CompilerParams(vmem_limit_bytes=VMEM_LIMIT),
            cost_estimate=pl.CostEstimate(
                flops=int(micros * PER_MICRO), bytes_accessed=1 << 20, transcendentals=0
            ),
        )(*[value for _, value, _ in self.ins])
        return SimpleNamespace(**dict(zip([item[0] for item in self.outs], outcome)))


def mask_into(pair_row, pair_col, mask_ref):
    mask_ref[...] = jnp.where(pair_col[...] == pair_row[...], 0.0, -1e30)


def lane_half(rows):
    return lax.broadcasted_iota(jnp.int32, (rows, SLAB), 1) < HD


def project(x_ref, weight, query_bias, value_bias, qkv_ref):
    for part, bias in enumerate((query_bias, None, value_bias)):
        at = pl.ds(part * D, D)
        made = mm(x_ref[...], weight[:, at])
        if bias is not None:
            made = made + vector(bias)
        qkv_ref[:, at] = made.astype(LOW)


def attend(qkv_ref, mask_ref, probs_ref, mixed_ref):
    first = lane_half(SEQ)

    @pl.loop(0, H // 2, unroll=True)
    def _(slab):
        queries = qkv_ref[:, columns(slab, SLAB)] * jnp.asarray(HD ** (-0.5), LOW)
        keys = qkv_ref[:, columns(slab + D // SLAB, SLAB)]
        values_t = qkv_ref[:, columns(slab + 2 * D // SLAB, SLAB)].T
        zero = jnp.zeros_like(keys)
        mixed = []
        for half in range(2):
            own = jnp.where(first, keys, zero) if half == 0 else jnp.where(first, zero, keys)
            scores = mm_nt(own, queries) + mask_ref[...]
            raised = jnp.exp(scores - jnp.max(scores, axis=0, keepdims=True))
            probs = (raised * (1.0 / jnp.sum(raised, axis=0, keepdims=True))).astype(LOW)
            if probs_ref is not None:
                probs_ref[2 * slab + half] = probs
            mixed.append(mm(values_t[half * HD : (half + 1) * HD], probs))
        mixed_ref[:, columns(slab, SLAB)] = jnp.concatenate(mixed, axis=0).T.astype(LOW)


def attend_back(qkv_ref, probs_ref, mixed_grad_ref, grad_ref):
    first = lane_half(SEQ)

    @pl.loop(0, H // 2, unroll=True)
    def _(slab):
        queries = qkv_ref[:, columns(slab, SLAB)] * jnp.asarray(HD ** (-0.5), LOW)
        keys_t = qkv_ref[:, columns(slab + D // SLAB, SLAB)].T
        values = qkv_ref[:, columns(slab + 2 * D // SLAB, SLAB)]
        grads = mixed_grad_ref[:, columns(slab, SLAB)]
        zero = jnp.zeros_like(values)
        query_grad, key_grad, value_grad = [], [], []
        for half in range(2):
            own = jnp.where(first, values, zero) if half == 0 else jnp.where(first, zero, values)
            probs = probs_ref[2 * slab + half]
            high = probs.astype(HIGH)
            product = high * mm_nt(own, grads)
            delta = jnp.sum(product, axis=0, keepdims=True)
            score_grad = (product - high * delta).astype(LOW)
            value_grad.append(mm(probs, grads))
            key_grad.append(mm(score_grad, queries))
            query_grad.append(mm(keys_t[half * HD : (half + 1) * HD], score_grad))
        grad_ref[:, columns(slab, SLAB)] = (
            jnp.concatenate(query_grad, axis=0).T * HD ** (-0.5)
        ).astype(LOW)
        grad_ref[:, columns(slab + D // SLAB, SLAB)] = jnp.where(first, *key_grad).astype(LOW)
        grad_ref[:, columns(slab + 2 * D // SLAB, SLAB)] = jnp.where(first, *value_grad).astype(LOW)


def first_norm(n, x, mixed):
    residual = x.astype(HIGH) + (mm(mixed, n.w_out[...]) + vector(n.out_bias))
    normed, inverse = normalize(residual)
    return normed, inverse, normed * vector(n.gain1) + vector(n.bias1)


def activate(n, low, act_ref, slope_ref):
    @pl.loop(0, FF // WIDE, unroll=True)
    def _(step):
        at = columns(step)
        before = mm(low, n.w_up[:, at]) + n.up_bias[:, at].astype(HIGH)
        share, bell = gelu_parts(before)
        act_ref[:, at] = (before * share).astype(LOW)
        if slope_ref is not None:
            slope_ref[:, at] = (share + before * bell * 0.3989422804014327).astype(LOW)


def second_norm(n, hidden, act):
    return normalize(hidden + (mm(act, n.w_down[...]) + vector(n.down_bias)))


def layer_out(n, normed):
    return (normed * vector(n.gain2) + vector(n.bias2)).astype(LOW)


def feed_back(n, branch_grad, slope_ref, pre_grad_ref):
    @pl.loop(0, FF // WIDE, unroll=True)
    def _(step):
        at = columns(step)
        act_grad = mm_nt(branch_grad, n.w_down[at, :])
        pre_grad_ref[:, at] = (act_grad * slope_ref[:, at].astype(HIGH)).astype(LOW)


def start_attention(place, x, pair_row, pair_col, vectors, pieces):
    rows = x.shape[0]
    k = Kernel(place)
    k.take(x=x, pair_row=pair_row, pair_col=pair_col)
    k.take(query_bias=vectors.query_bias, value_bias=vectors.value_bias)
    k.take_matrix(qkv=pieces.qkv)
    k.give(mixed=((rows, SEQ, D), LOW))
    k.hold(mask=((SEQ, SEQ), HIGH), qkv=STATE["qkv"])

    def body(n, copies):
        n.load(n.w_qkv)
        for row in range(rows):
            mask_into(n.pair_row.at[row], n.pair_col.at[row], n.mask)
            copies.ready(n.w_qkv)
            project(n.x.at[row], n.w_qkv, n.query_bias, n.value_bias, n.qkv)
            attend(n.qkv, n.mask, None, n.mixed.at[row])

    return k.run(body, 14).mixed


def start_middle(place, row, x, mixed, vectors, pieces):
    k = Kernel(place)
    k.pull_row(row, x=x, mixed=mixed)
    k.take(out_bias=vectors.out_bias, gain1=vectors.gain1)
    k.take(bias1=vectors.bias1, up_bias=vectors.up_bias)
    k.take_matrix(out=pieces.out, up=pieces.up)
    k.give(hidden=((SEQ, D), HIGH), act=((SEQ, FF), LOW))

    def body(n, copies):
        n.fetch(n.x, n.mixed)
        n.load(n.w_out, n.w_up)
        copies.ready(n.x, n.mixed, n.w_out)
        _, _, hidden = first_norm(n, n.x[...], n.mixed[...])
        n.hidden[...] = hidden
        copies.ready(n.w_up)
        activate(n, hidden.astype(LOW), n.act, None)

    outcome = k.run(body, 8)
    return outcome.hidden, outcome.act


def start_last(place, hidden, act, vectors, pieces):
    k = Kernel(place)
    k.take(hidden=hidden, act=act)
    k.take(down_bias=vectors.down_bias, gain2=vectors.gain2, bias2=vectors.bias2)
    k.take_matrix(down=pieces.down)
    k.give(out=((SEQ, D), LOW))

    def body(n, copies):
        n.load(n.w_down)
        copies.ready(n.w_down)
        n.out[...] = layer_out(n, second_norm(n, n.hidden[...], n.act[...])[0])

    return k.run(body, 6).out


def start_rest(place, row, x, mixed, vectors, pieces):
    k = Kernel(place)
    k.pull_row(row, x=x, mixed=mixed)
    k.take(out_bias=vectors.out_bias, gain1=vectors.gain1, bias1=vectors.bias1)
    k.take(up_bias=vectors.up_bias, down_bias=vectors.down_bias)
    k.take(gain2=vectors.gain2, bias2=vectors.bias2)
    k.take_matrix(out=pieces.out, up=pieces.up, down=pieces.down)
    k.give(out=((SEQ, D), LOW))
    k.hold(hidden=((SEQ, D), HIGH), act=((SEQ, FF), LOW))

    def body(n, copies):
        n.fetch(n.x, n.mixed)
        n.load(n.w_out, n.w_up, n.w_down)
        copies.ready(n.x, n.mixed, n.w_out)
        _, _, hidden = first_norm(n, n.x[...], n.mixed[...])
        n.hidden[...] = hidden
        copies.ready(n.w_up)
        activate(n, hidden.astype(LOW), n.act, None)
        copies.ready(n.w_down)
        n.out[...] = layer_out(n, second_norm(n, n.hidden[...], n.act[...])[0])

    return k.run(body, 10).out


def there_and_back(
    place, row, tokens, handed, gradient, pair_row, pair_col, vectors, pieces, before=None
):
    k = Kernel(place)
    k.pull_row(row, tokens=tokens, gradient=gradient)
    k.pull(handed=handed)
    k.take(pair_row=pair_row, pair_col=pair_col)
    k.take(**vars(vectors))
    k.take_matrix(**vars(pieces))
    k.give(out=((row + 1, SEQ, D), LOW), in_grad=((SEQ, D), LOW))
    if before is not None:
        k.take(before=before)
    k.give_far(**{"kept_" + name: like for name, like in STATE.items()})
    k.hold(**STATE)
    k.hold(
        resid=((SEQ, D), HIGH),
        pre_grad=((SEQ, FF), LOW),
        mixed_grad=((SEQ, D), LOW),
        proj_grad=((SEQ, 3 * D), LOW),
        mask=((SEQ, SEQ), HIGH),
    )

    def body(n, copies):
        def keep(**values):
            for name, value in values.items():
                if value is not None:
                    getattr(n, name)[...] = value
                copies.start(None, getattr(n, name), getattr(n, "kept_" + name))

        n.fetch(n.tokens, n.handed)
        n.load(n.w_qkv, n.w_out, n.w_up, n.w_down)
        n.fetch(n.gradient)
        copies.ready(n.tokens, n.handed)
        keep(x=jnp.where(n.place[2] == 0, n.tokens[...], n.handed[...]))
        mask_into(n.pair_row.at[row], n.pair_col.at[row], n.mask)
        copies.ready(n.w_qkv)
        project(n.x, n.w_qkv, n.query_bias, n.value_bias, n.qkv)
        keep(qkv=None)
        attend(n.qkv, n.mask, n.probs, n.mixed)
        keep(probs=None, mixed=None)
        copies.ready(n.w_out)
        normed, inverse, hidden = first_norm(n, n.x[...], n.mixed[...])
        n.resid[...] = hidden
        keep(normed1=normed, inverse1=inverse, low=hidden.astype(LOW))
        copies.ready(n.w_up)
        activate(n, n.low[...], n.act, n.slope)
        keep(act=None, slope=None)
        copies.ready(n.w_down)
        normed, inverse = second_norm(n, n.resid[...], n.act[...])
        keep(normed2=normed, inverse2=inverse)
        n.out[row] = layer_out(n, normed)
        if before is not None:
            n.out[:row] = n.before[...]

        copies.ready(n.gradient)
        resid = norm_back(
            n.gradient[...].astype(HIGH), n.normed2[...], n.inverse2[...], vector(n.gain2)
        )
        n.resid[...] = resid
        feed_back(n, resid.astype(LOW), n.slope, n.pre_grad)
        hidden_grad = n.resid[...] + mm_nt(n.pre_grad[...], n.w_up[...])
        resid = norm_back(hidden_grad, n.normed1[...], n.inverse1[...], vector(n.gain1))
        n.resid[...] = resid
        n.mixed_grad[...] = mm_nt(resid.astype(LOW), n.w_out[...]).astype(LOW)
        attend_back(n.qkv, n.probs, n.mixed_grad, n.proj_grad)
        n.in_grad[...] = (n.resid[...] + mm_nt(n.proj_grad[...], n.w_qkv[...])).astype(LOW)

    outcome = k.run(body, 27)
    state = {name: getattr(outcome, "kept_" + name) for name in STATE}
    return outcome.out, outcome.in_grad, state


def take_rows(k, states, *names):
    for name in names:
        shape, kind = STATE[name]
        k.take_far(**{f"{name}_{row}": state[name] for row, state in enumerate(states)})
        k.hold(**{name: ((len(states) * shape[0], *shape[1:]), kind)})
        k.sems += len(states)


def fetch_rows(n, copies, **targets):
    for name, target in targets.items():
        length = STATE[name][0][0]
        for row in range(target.shape[0] // length):
            part = target.at[pl.ds(row * length, length)]
            copies.start(target, getattr(n, f"{name}_{row}"), part)


def parts_of(outcome):
    found = vars(outcome)
    return [(found["sent" + name[4:]], found[name]) for name in found if name[:4] == "kept"]


def send_blocks(n, copies):
    copies.blocks(n.place, n.stage, parts_of(n))


def product(stage, left, right):
    @pl.loop(0, stage.shape[1] // WIDE, unroll=True)
    def _(step):
        at = columns(step)
        stage[:, at] = mm_tn(left[...], right[:, at]).astype(LOW)


def pull_halves(k, **arrays):
    for name, value in arrays.items():
        k.take_far(**{"first_" + name: value})
        k.hold(**{name: ((2 * SEQ, *value.shape[1:]), value.dtype)})
        k.sems += 1


def fetch_halves(n, copies, **targets):
    for name, target in targets.items():
        copies.start(target, getattr(n, "first_" + name), target.at[pl.ds(0, SEQ)])


def add_sums(sums, at, **values):
    for value in values.values():
        put = slice(at, at + value.shape[1])
        sums[:, put] = sums[:, put] + value
        at += value.shape[1]


def feed_sums(sums, at, pre_grad, hidden_grad, normed, mixer_grad):
    add_sums(
        sums,
        at,
        up_bias=column_sum(pre_grad),
        gain1=column_sum(hidden_grad * normed),
        bias1=column_sum(hidden_grad),
        out_bias=column_sum(mixer_grad),
    )


def norm_sums(sums, gradient, normed, branch_grad):
    add_sums(
        sums,
        0,
        gain2=column_sum(gradient * normed),
        bias2=column_sum(gradient),
        down_bias=column_sum(branch_grad),
    )


def projection_sums(sums, proj_grad):
    add_sums(
        sums,
        SUMS_WIDTH - 2 * D,
        query_bias=column_sum(proj_grad[:, :D]),
        value_bias=column_sum(proj_grad[:, 2 * D :]),
    )


def back_first(place, cotangent, handed, state, vectors, pieces):
    k = Kernel(place)
    k.pull_row(0, cotangent=cotangent)
    k.pull(handed=handed)
    k.take(gain1=vectors.gain1, gain2=vectors.gain2)
    k.take_matrix(down=pieces.down, up=pieces.up)
    names = ("normed2", "inverse2", "slope", "normed1", "inverse1")
    k.pull(**{name: state[name] for name in names})
    k.put(
        branch_grad=((SEQ, D), LOW),
        pre_grad=((SEQ, FF), LOW),
        mixer_grad=((SEQ, D), LOW),
        resid=((SEQ, D), HIGH),
    )
    k.give(sums=((1, SUMS_WIDTH), HIGH))

    def body(n, copies):
        n.fetch(n.handed, n.cotangent, n.normed2, n.inverse2)
        n.load(n.w_down)
        n.fetch(n.slope)
        n.load(n.w_up)
        n.fetch(n.normed1, n.inverse1)
        n.sums[...] = jnp.zeros_like(n.sums)
        copies.ready(n.handed, n.cotangent, n.normed2, n.inverse2)
        gradient = jnp.where(n.place[2] == 0, n.handed[...], n.cotangent[...]).astype(HIGH)
        normed = n.normed2[...]
        resid = norm_back(gradient, normed, n.inverse2[...], vector(n.gain2))
        n.resid[...] = resid
        n.branch_grad[...] = resid.astype(LOW)
        n.send(n.branch_grad)
        norm_sums(n.sums, gradient, normed, n.branch_grad[...])
        copies.ready(n.w_down, n.slope)
        feed_back(n, n.branch_grad[...], n.slope, n.pre_grad)
        n.send(n.pre_grad)
        copies.ready(n.w_up, n.normed1, n.inverse1)
        hidden_grad = n.resid[...] + mm_nt(n.pre_grad[...], n.w_up[...])
        normed = n.normed1[...]
        resid = norm_back(hidden_grad, normed, n.inverse1[...], vector(n.gain1))
        n.resid[...] = resid
        n.mixer_grad[...] = resid.astype(LOW)
        n.send(n.mixer_grad, n.resid)
        feed_sums(n.sums, 3 * D, n.pre_grad[...], hidden_grad, normed, n.mixer_grad[...])

    return k.run(body, 9)


def back_down(place, cotangent, handed, first, states, vectors):
    k = Kernel(place)
    k.pull_row(1, cotangent=cotangent)
    k.pull(handed=handed)
    k.take(gain2=vectors.gain2, first_sums=first.sums)
    k.pull(normed2=states[1]["normed2"], inverse2=states[1]["inverse2"])
    take_rows(k, states, "act")
    pull_halves(k, branch_grad=first.to_branch_grad)
    k.put(resid=((SEQ, D), HIGH))
    k.give_far(second_grad=((SEQ, D), LOW))
    k.give(sums=((1, SUMS_WIDTH), HIGH))
    half = FF // 8
    for part in range(2):
        k.give_far(**{f"sent{part}": ((half, 2 * D), LOW), f"kept{part}": ((half, 2 * D), LOW)})
        k.sems += 8
    k.hold(stage=((8 * half, D), LOW))

    def body(n, copies):
        n.fetch(n.handed, n.cotangent, n.normed2, n.inverse2)
        fetch_halves(n, copies, branch_grad=n.branch_grad)
        fetch_rows(n, copies, act=n.act)
        n.sums[...] = n.first_sums[...]
        copies.ready(n.handed, n.cotangent, n.normed2, n.inverse2)
        second = pl.ds(SEQ, SEQ)
        gradient = jnp.where(n.place[2] == 0, n.handed[...], n.cotangent[...]).astype(HIGH)
        normed = n.normed2[...]
        resid = norm_back(gradient, normed, n.inverse2[...], vector(n.gain2))
        n.resid[...] = resid
        n.branch_grad[second, :] = resid.astype(LOW)
        norm_sums(n.sums, gradient, normed, n.branch_grad[second, :])
        n.send(n.resid)
        copies.start(None, n.branch_grad.at[second, :], n.second_grad)
        copies.ready(n.act, n.branch_grad)
        for part, (sent, kept) in enumerate(parts_of(n)):
            for number in (1, 3, 0, 2):
                start = (n.place[0] ^ number) * (2 * half) + part * half
                at = pl.ds(pl.multiple_of(start, half), half)
                put = (4 * part + number) * half
                n.stage[pl.ds(put, half), :] = mm_tn(n.act[:, at], n.branch_grad[...]).astype(LOW)
                target, short = (kept, sent)[number % 2], half // 2
                for side in range(2):
                    into = target.at[pl.ds(number // 2 * short, short), pl.ds(side * D, D)]
                    copies.start(target, n.stage.at[pl.ds(put + side * short, short), :], into)

    outcome = k.run(body, 8)
    return outcome, parts_of(outcome)


def swap(value, axis, bit):
    devices = lax.axis_size(axis)
    return lax.ppermute(value, axis, [(i, i ^ bit) for i in range(devices)])


def half_of(shard):
    rows = shard.shape[0] // 2
    return lax.dynamic_slice_in_dim(shard, lax.axis_index("dp") % 2 * rows, rows, axis=0)


def all_pieces(shard, far, other):
    return [shard, far, other, swap(shard, "rep", 1), swap(far, "rep", 1), swap(other, "rep", 1)]


def add_low(*values):
    total = values[0].astype(HIGH)
    for value in values[1:]:
        total = total + value.astype(HIGH)
    return total.astype(LOW)


def after(value, *others):
    others = [other for other in others if other is not None]
    return lax.optimization_barrier((value, *others))[0] if others else value


def fit(value, shape):
    return jnp.pad(value, [(0, want - have) for want, have in zip(shape, value.shape)])


def common(first, second):
    return tuple(max(pair) for pair in zip(first.shape, second.shape))


class Reduction:
    def __init__(self):
        self.x, self.ends, self.across = [], [], []
        self.totals, self.finals = [], []
        self.waiting, self.payload = [], ()
        index = lax.axis_index("dp")
        self.line = lax.axis_size("dp") == 4
        self.edge = (index == 0) | (index == 3)

    def start(self, own, far, *deps):
        self.x.append(swap(after(far, *self.x[-1:], *deps), "rep", 2))
        total = add_low(*own, self.x[-1])
        if self.line:
            self.waiting.append(total)
        else:
            self.finals.append(lax.psum(total, "dp").astype(HIGH))

    def step(self, *deps):
        if self.line:
            self.turn(after(self.waiting.pop(0), *deps))

    def turn(self, total):
        at = len(self.ends)
        back = self.totals[at - BACK] if at >= BACK else None
        if total is None or back is None:
            payload = back if total is None else total
        else:
            shape = common(total, back)
            payload = jnp.where(self.edge, fit(total, shape), fit(back, shape))
        self.payload = (payload,)
        arrived = swap(after(payload, *self.ends[-1:]), "dp", 1)
        self.ends.append(arrived)
        if back is not None:
            here = arrived[: back.shape[0], : back.shape[1]]
            self.finals.append(jnp.where(self.edge, here, back).astype(HIGH))
        if total is not None:
            sums = add_low(total, arrived[: total.shape[0], : total.shape[1]])
            self.across.append(
                lax.ppermute(sums, "dp", [(1, 2), (2, 1)])
            )
            self.totals.append(add_low(sums, self.across[-1]))

    def finish(self):
        if self.line:
            for _ in range(BACK):
                self.turn(None)
        return self.finals


def between_cores(parts):
    own, far = [], []
    for sent, kept in parts:
        rows = kept.shape[0] // 2
        arrived = swap(sent, "rep", 1)
        own.append((kept[:rows], arrived[:rows]))
        far.append((kept[rows:], arrived[rows:]))
    return own, far


def spread(value):
    index = lax.axis_index("rep")
    for bit in (1, 2):
        other = swap(value, "rep", bit)
        high = (index & bit) > 0
        value = jnp.concatenate([jnp.where(high, other, value), jnp.where(high, value, other)])
    return value


def segment_ids(lengths):
    bounds = jnp.cumsum(lengths, axis=-1)
    places = jnp.arange(SEQ, dtype=jnp.int32)
    return jnp.sum((places[None, :, None] >= bounds[:, None, :]).astype(jnp.int32), axis=-1)


def per_device(
    tokens,
    cotangent,
    pair_lengths,
    qkv_weight,
    out_weight,
    up_weight,
    down_weight,
    query_bias,
    value_bias,
    out_bias,
    norm1_gain,
    norm1_bias,
    up_bias,
    down_bias,
    norm2_gain,
    norm2_bias,
):
    rows = tokens.shape[0]
    place = jnp.stack(
        [lax.axis_index("rep"), lax.axis_index("dp") % 2, lax.axis_index("section")]
    ).astype(jnp.int32)
    vectors = SimpleNamespace(
        query_bias=query_bias,
        value_bias=value_bias,
        out_bias=out_bias,
        gain1=norm1_gain,
        bias1=norm1_bias,
        up_bias=up_bias,
        down_bias=down_bias,
        gain2=norm2_gain,
        bias2=norm2_bias,
    )
    pairs = segment_ids(pair_lengths)
    pair_row, pair_col = pairs[:, None, :], pairs[:, :, None]

    shards = SimpleNamespace(
        qkv=qkv_weight[0],
        mid=jnp.concatenate([out_weight[0], up_weight[0]], axis=1),
        down=down_weight[0],
    )
    far, other, pieces = SimpleNamespace(), SimpleNamespace(), SimpleNamespace()
    far.qkv = swap(half_of(shards.qkv), "rep", 2)
    other.qkv = swap(far.qkv, "dp", 1)
    pieces.qkv = all_pieces(shards.qkv, far.qkv, other.qkv)
    far.mid = swap(after(half_of(shards.mid), far.qkv), "rep", 2)
    mixed = start_attention(after(place, far.mid), tokens, pair_row, pair_col, vectors, pieces)
    other.mid = swap(far.mid, "dp", 1)
    far.down = swap(after(half_of(shards.down), far.mid), "rep", 2)
    pieces.up = all_pieces(shards.mid, far.mid, after(other.mid, mixed, far.down))
    pieces.out = pieces.up
    other.down = swap(after(far.down, other.mid, mixed), "dp", 1)
    hidden, act = start_middle(place, 0, tokens, mixed, vectors, pieces)
    pieces.down = all_pieces(shards.down, far.down, after(other.down, act))
    out = start_last(place, hidden, act, vectors, pieces)
    handed = [lax.ppermute(out, "section", [(0, 1)])]
    out = start_rest(after(place, out), 1, tokens, mixed, vectors, pieces)
    handed.append(lax.ppermute(out, "section", [(0, 1)]))

    out, states, handed_back = None, [], []
    for row in range(rows):
        out, in_grad, state = there_and_back(
            place, row, tokens, handed[row], cotangent, pair_row, pair_col, vectors, pieces, out
        )
        states.append(state)
        handed_back.append(lax.ppermute(in_grad, "section", [(1, 0)]))

    reduction = Reduction()
    first = back_first(place, cotangent, handed_back[0], states[0], vectors, pieces)
    fed, down_parts = back_down(place, cotangent, handed_back[1], first, states, vectors)
    own, far = between_cores(down_parts)
    fars = [add_low(*item) for item in far]
    hid = back_up(
        after(place, fars[0], fars[1]),
        fed.second_grad,
        fed.to_resid,
        fed.sums,
        first,
        states,
        vectors,
        pieces,
    )
    reduction.start(own[0], fars[0])
    sent_up = after(hid.sent_up, reduction.x[0])
    up_own, up_far = between_cores([(sent_up, hid.kept_up)])
    out_own, out_far = between_cores([(hid.sent_out, hid.kept_out)])
    reduction.start(own[1], fars[1])
    reduction.step()
    mix = back_mix(
        after(place, reduction.x[0]),
        (first.to_mixer_grad, hid.second_grad),
        (first.to_resid, hid.to_resid),
        hid.sums,
        states,
        pieces,
    )
    sent = after(mix.sent0, reduction.x[1], *reduction.ends[:1])
    own, far = between_cores([(sent, mix.kept0)])

    def beside(left, right):
        left = [jnp.pad(value, [(0, EXTRA), (0, 0)]) for value in left]
        return [jnp.concatenate([a, b[:, :D]], axis=1) for a, b in zip(left, right)]

    half = FF // 2
    reduction.start([v[:, :half] for v in up_own[0]], add_low(*[v[:, :half] for v in up_far[0]]))
    reduction.step()
    reduction.step(reduction.x[2])
    reduction.start(
        [v[:, half:] for v in up_own[0]], add_low(*[v[:, half:] for v in up_far[0]]), *reduction.payload
    )
    reduction.step(reduction.x[3])
    reduction.start(
        beside(out_own[0], own[0]), add_low(*beside(out_far[0], far[0])), *reduction.payload
    )
    reduction.step(reduction.x[4])
    tail = [[v[: D // 4, D:] for v in values] for values in (own[0], far[0])]
    reduction.start(tail[0], add_low(*tail[1]), *reduction.payload)
    reduction.step()
    down0, down1, up0, up1, beside, qkv = reduction.finish()
    block = beside[D // 4 :, D:]
    sums = spread(block[:3].reshape(3 * D).astype(LOW))[None].astype(HIGH)
    totals = [
        jnp.concatenate([beside[: D // 4, D:], qkv], axis=1),
        beside[: D // 4, :D],
        jnp.concatenate([up0, up1], axis=1),
        jnp.concatenate([down0[:, :D], down0[:, D:], down1[:, :D], down1[:, D:]], axis=0),
    ]
    vector_totals = [
        sums[:, SUM_AT[name][0] : SUM_AT[name][0] + SUM_AT[name][1]] for name in vars(vectors)
    ]
    return (
        out[None],
        mix.in_grad[None],
        *[total[None] for total in totals],
        *vector_totals,
    )


def solution(mesh):
    rows = P(("dp", "rep"), None, None)
    matrix = P("section", "rep", None)
    row = P("section", None)
    made = P("section", ("dp", "rep"), None, None)
    return jax.shard_map(
        per_device,
        mesh=mesh,
        in_specs=(rows, rows, P(("dp", "rep"), None)) + (matrix,) * 4 + (row,) * 9,
        out_specs=(made, made) + (matrix,) * 4 + (row,) * 9,
        check_vma=False,
    )
```

```python
from types import SimpleNamespace

import jax
import jax.numpy as jnp
from jax import lax
from jax.experimental import pallas as pl
from jax.experimental.pallas import tpu as pltpu
from jax.sharding import PartitionSpec as P

D = 768
H = 12
FF = 3072
HD = 64
SEQ = 256
SLAB = 128
WIDE = 768
HIGH = jnp.float32
LOW = jnp.bfloat16
VMEM_LIMIT = 56 << 20
PER_MICRO = 1_150_000_000


def mm(left, right):
    return lax.dot_general(left, right, (((1,), (0,)), ((), ())), preferred_element_type=HIGH)


def mm_nt(left, right):
    return lax.dot_general(left, right, (((1,), (1,)), ((), ())), preferred_element_type=HIGH)


def mm_tn(left, right):
    return lax.dot_general(left, right, (((0,), (0,)), ((), ())), preferred_element_type=HIGH)


def columns(step, width=WIDE):
    return pl.ds(pl.multiple_of(step * width, width), width)


def normalize(residual):
    center = jnp.mean(residual, axis=-1, keepdims=True)
    shifted = residual - center
    inverse = lax.rsqrt(jnp.mean(shifted * shifted, axis=-1, keepdims=True) + 1e-12)
    return shifted * inverse, inverse


def norm_back(gradient, normed, inverse, gain_row):
    scaled = gradient * gain_row
    return inverse * (
        scaled
        - jnp.mean(scaled, axis=-1, keepdims=True)
        - normed * jnp.mean(scaled * normed, axis=-1, keepdims=True)
    )


def gelu_parts(u):
    t = 1.0 / (1.0 + 0.23164188 * jnp.abs(u))
    tail = t * (
        0.127414796 + t * (-0.142248368 + t * (0.7107068705 + t * (-0.7265760135 + t * 0.5307027145)))
    )
    bell = jnp.exp(u * u * -0.5)
    tail = tail * bell
    return jnp.where(u < 0.0, tail, 1.0 - tail), bell


def column_sum(value):
    return jnp.sum(value.astype(HIGH), axis=0, keepdims=True)


def vector(ref):
    return ref[...].astype(HIGH)


FULL = dict(qkv=(D, 3 * D), out=(D, D), up=(D, FF), down=(FF, D))
STATE = dict(
    x=((SEQ, D), LOW),
    qkv=((SEQ, 3 * D), LOW),
    probs=((H, SEQ, SEQ), LOW),
    mixed=((SEQ, D), LOW),
    normed1=((SEQ, D), HIGH),
    inverse1=((SEQ, 1), HIGH),
    low=((SEQ, D), LOW),
    slope=((SEQ, FF), LOW),
    act=((SEQ, FF), LOW),
    normed2=((SEQ, D), HIGH),
    inverse2=((SEQ, 1), HIGH),
)
SUMS = dict(
    gain2=D, bias2=D, down_bias=D, up_bias=FF, gain1=D, bias1=D, out_bias=D, query_bias=D, value_bias=D
)
SUM_AT = {}
for _name in SUMS:
    SUM_AT[_name] = (sum(width for _, width in SUM_AT.values()), SUMS[_name])
PIECES = 6
COLUMN = dict(out=0, up=D)
SUMS_WIDTH = sum(SUMS.values())
EXTRA = 16
BACK = 2


class Copies:
    def __init__(self, sems):
        self.sems, self.flying, self.used = sems, {}, 0

    def start(self, key, source, target):
        copy = pltpu.make_async_copy(source, target, self.sems.at[self.used])
        self.used += 1
        copy.start()
        self.flying.setdefault(id(key), []).append(copy)

    def ready(self, *keys):
        for key in keys:
            for copy in self.flying.pop(id(key), ()):
                copy.wait()

    def by_blocks(self, place, target):
        rows = target.shape[0] // 4
        pieces = self.flying.pop(id(target), [])
        for number, count in ((0, 1), (2, 2), (1, 1), (3, 2)):
            for copy in pieces[:count]:
                copy.wait()
            pieces = pieces[count:]
            yield pl.ds(pl.multiple_of((place[0] ^ number) * rows, rows), rows)

    def finish(self):
        for key in list(self.flying):
            for copy in self.flying.pop(key):
                copy.wait()

    def matrix(self, place, pieces, target, column):
        own, half = place[0], place[1]
        rows = target.shape[0] // 4
        short = rows // 2
        starts = []
        for near in range(2):
            starts.append((own ^ near) * rows)
            starts.append((own ^ (near + 2)) * rows + half * short)
            starts.append((own ^ (near + 2)) * rows + (1 - half) * short)
        for source, start in zip(pieces, starts):
            at = pl.ds(pl.multiple_of(start, 16), source.shape[0])
            if column is not None:
                source = source.at[:, pl.ds(column, target.shape[1])]
            self.start(target, source, target.at[at, :])

    def blocks(self, place, stage, parts):
        rows, column = stage.shape[0] // 4, 0
        for sent, kept in parts:
            width = sent.shape[1]
            for number in (1, 3, 0, 2):
                at = pl.ds(pl.multiple_of((place[0] ^ number) * rows, 16), rows)
                put = pl.ds(number // 2 * (sent.shape[0] // 2), rows)
                target = (kept, sent)[number % 2].at[put, :]
                self.start(target, stage.at[at, pl.ds(column, width)], target)
            column += width


def back_up(place, branch_grad, resid, sums, first, states, vectors, pieces):
    second = pl.ds(SEQ, SEQ)
    k = Kernel(place)
    k.pull(branch_grad=branch_grad, old_resid=resid)
    k.take(gain1=vectors.gain1, old_sums=sums)
    k.take_matrix(down=pieces.down, up=pieces.up)
    names = ("slope", "normed1", "inverse1")
    k.pull(**{name: states[1][name] for name in names})
    take_rows(k, states, "low", "mixed")
    pull_halves(k, pre_grad=first.to_pre_grad, mixer_grad=first.to_mixer_grad)
    k.put(resid=((SEQ, D), HIGH))
    k.give_far(second_grad=((SEQ, D), LOW))
    k.give(sums=((1, SUMS_WIDTH), HIGH))
    for name, width in (("up", FF), ("out", D)):
        shape = ((D // 2, width), LOW)
        k.give_far(**{"sent_" + name: shape, "kept_" + name: shape})
        k.hold(**{"stage_" + name: ((D, width), LOW)})
        k.sems += 2

    def body(n, copies):
        n.fetch(n.branch_grad)
        n.fetch(n.slope)
        n.load(n.w_down)
        fetch_halves(n, copies, pre_grad=n.pre_grad)
        fetch_rows(n, copies, low=n.low)
        n.load(n.w_up)
        n.fetch(n.old_resid, n.normed1, n.inverse1)
        fetch_halves(n, copies, mixer_grad=n.mixer_grad)
        fetch_rows(n, copies, mixed=n.mixed)
        n.sums[...] = n.old_sums[...]
        copies.ready(n.branch_grad, n.slope)
        feed_back(n, copies, n.branch_grad[...], n.slope, n.pre_grad.at[second, :])
        copies.ready(n.low, n.pre_grad)
        product(n.stage_up, n.low, n.pre_grad)
        copies.blocks(n.place, n.stage_up, [(n.sent_up, n.kept_up)])
        copies.ready(n.w_up, n.old_resid, n.normed1, n.inverse1)
        hidden_grad = n.old_resid[...] + mm_nt(n.pre_grad[second, :], n.w_up[...])
        normed = n.normed1[...]
        resid = norm_back(hidden_grad, normed, n.inverse1[...], vector(n.gain1))
        n.resid[...] = resid
        n.mixer_grad[second, :] = resid.astype(LOW)
        n.send(n.resid)
        copies.start(None, n.mixer_grad.at[second, :], n.second_grad)
        feed_sums(
            n.sums, 3 * D, n.pre_grad[second, :], hidden_grad, normed, n.mixer_grad[second, :]
        )
        copies.ready(n.mixed, n.mixer_grad)
        product(n.stage_out, n.mixed, n.mixer_grad)
        copies.blocks(n.place, n.stage_out, [(n.sent_out, n.kept_out)])

    return k.run(body, 14)


def back_mix(place, mixer_grads, resids, sums, states, pieces):
    k = Kernel(place)
    k.pull(mixer0=mixer_grads[0], mixer1=mixer_grads[1], resid0=resids[0], resid1=resids[1])
    k.take(old_sums=sums)
    k.take_matrix(out=pieces.out, qkv=pieces.qkv)
    take_rows(k, states, "qkv", "probs", "x")
    k.hold(mixed_grad=((SEQ, D), LOW), proj_grad=((2 * SEQ, 3 * D), LOW))
    k.hold(sums=((1, SUMS_WIDTH), HIGH), sums_stage=((4 * EXTRA, 3 * D), LOW))
    k.hold(stage=((D, 3 * D), LOW))
    k.give(in_grad=((2, SEQ, D), LOW))
    shape = ((D // 2 + 2 * EXTRA, 3 * D), LOW)
    k.give_far(sent0=shape, kept0=shape)
    k.sems += 8

    def body(n, copies):
        n.fetch(n.mixer0)
        n.load(n.w_out)
        fetch_rows(n, copies, qkv=n.qkv, probs=n.probs)
        n.fetch(n.mixer1)
        fetch_rows(n, copies, x=n.x)
        n.load(n.w_qkv)
        n.fetch(n.resid0, n.resid1)
        n.sums[...] = n.old_sums[...]
        copies.ready(n.w_out)
        for row, mixer_grad in enumerate((n.mixer0, n.mixer1)):
            at = pl.ds(row * SEQ, SEQ)
            copies.ready(mixer_grad)
            n.mixed_grad[...] = mm_nt(mixer_grad[...], n.w_out[...]).astype(LOW)
            copies.ready(n.qkv, n.probs)
            probs = n.probs.at[pl.ds(row * H, H)]
            attend_back(n.qkv.at[at, :], probs, n.mixed_grad, n.proj_grad.at[at, :])
        copies.ready(n.x)
        product(n.stage, n.x, n.proj_grad)
        send_blocks(n, copies)
        projection_sums(n.sums, n.proj_grad)
        quarter = SUMS_WIDTH // 4
        n.sums_stage[...] = jnp.zeros_like(n.sums_stage)
        for number in (1, 3, 0, 2):
            start = (n.place[0] ^ number) * quarter
            own = n.sums[:, pl.ds(pl.multiple_of(start, SLAB), quarter)].astype(LOW)
            base = number * EXTRA
            for line in range(3):
                piece = own[:, line * D : (line + 1) * D]
                n.sums_stage[base + line : base + line + 1, :D] = piece
            target = (n.kept0, n.sent0)[number % 2]
            block = target.shape[0] // 2
            put = pl.ds((number // 2 + 1) * block - EXTRA, EXTRA)
            copies.start(target, n.sums_stage.at[pl.ds(base, EXTRA), :], target.at[put, :])
        copies.ready(n.w_qkv)
        for row, resid in enumerate((n.resid0, n.resid1)):
            at = pl.ds(row * SEQ, SEQ)
            copies.ready(resid)
            total = resid[...] + mm_nt(n.proj_grad[at, :], n.w_qkv[...])
            n.in_grad[row] = total.astype(LOW)

    return k.run(body, 14)


class Kernel:
    def __init__(self, place):
        self.ins, self.outs, self.scratch, self.sems = [], [], [], 0
        self.matrices, self.rows = [], {}
        self.add_in(pltpu.SMEM, place=place)

    def add_in(self, space, **arrays):
        for name, value in arrays.items():
            self.ins.append((name, value, pl.BlockSpec(memory_space=space)))

    def take(self, **arrays):
        self.add_in(pltpu.VMEM, **arrays)

    def take_far(self, **arrays):
        self.add_in(pl.ANY, **arrays)

    def take_matrix(self, **matrices):
        for name, pieces in matrices.items():
            self.matrices.append(name)
            self.take_far(**{f"{name}{number}": piece for number, piece in enumerate(pieces)})
            self.hold(**{"w_" + name: (FULL[name], LOW)})
            self.sems += len(pieces)

    def add_out(self, space, shapes):
        for name, (shape, kind) in shapes.items():
            spec = pl.BlockSpec(memory_space=space)
            self.outs.append((name, jax.ShapeDtypeStruct(shape, kind), spec))

    def give(self, **shapes):
        self.add_out(pltpu.VMEM, shapes)

    def give_far(self, **shapes):
        self.add_out(pl.ANY, shapes)
        self.sems += len(shapes)

    def hold(self, **shapes):
        self.scratch += [(name, pltpu.VMEM(shape, kind)) for name, (shape, kind) in shapes.items()]

    def pull(self, **arrays):
        for name, value in arrays.items():
            self.take_far(**{"from_" + name: value})
            self.hold(**{name: (value.shape, value.dtype)})
            self.sems += 1

    def pull_row(self, row, **arrays):
        for name, value in arrays.items():
            self.take_far(**{"from_" + name: value})
            self.hold(**{name: (value.shape[1:], value.dtype)})
            self.sems += 1
            self.rows[name] = row

    def put(self, **shapes):
        for name, like in shapes.items():
            self.give_far(**{"to_" + name: like})
            self.hold(**{name: like})

    def run(self, body, micros, sems=0):
        names = [item[0] for item in self.ins + self.outs + self.scratch]

        def kernel(*refs):
            n = SimpleNamespace(**dict(zip(names, refs[:-1])))
            copies = Copies(refs[-1])

            def load(*wanted):
                for target in wanted:
                    for name in self.matrices:
                        if getattr(n, "w_" + name) is target:
                            pieces = [getattr(n, f"{name}{number}") for number in range(PIECES)]
                            copies.matrix(n.place, pieces, target, COLUMN.get(name))

            def move(prefix, source_first):
                def start(*wanted):
                    for target in wanted:
                        for name, ref in vars(n).items():
                            if ref is target:
                                other = getattr(n, prefix + name)
                                if source_first and name in self.rows:
                                    other = other.at[self.rows[name]]
                                pair = (other, target) if source_first else (target, other)
                                copies.start(target, *pair)

                return start

            n.load, n.fetch, n.send = load, move("from_", True), move("to_", False)
            body(n, copies)
            copies.finish()

        outcome = pl.pallas_call(
            kernel,
            in_specs=[spec for _, _, spec in self.ins],
            out_specs=[spec for _, _, spec in self.outs],
            out_shape=[shape for _, shape, _ in self.outs],
            scratch_shapes=[item[1] for item in self.scratch]
            + [pltpu.SemaphoreType.DMA((self.sems + sems,))],
            compiler_params=pltpu.CompilerParams(vmem_limit_bytes=VMEM_LIMIT),
            cost_estimate=pl.CostEstimate(
                flops=int(micros * PER_MICRO), bytes_accessed=1 << 20, transcendentals=0
            ),
        )(*[value for _, value, _ in self.ins])
        return SimpleNamespace(**dict(zip([item[0] for item in self.outs], outcome)))


def mask_into(pair_row, pair_col, mask_ref):
    mask_ref[...] = jnp.where(pair_col[...] == pair_row[...], 0.0, -1e30)


def lane_half(rows):
    return lax.broadcasted_iota(jnp.int32, (rows, SLAB), 1) < HD


def project(x_ref, weight, query_bias, value_bias, qkv_ref):
    for part, bias in enumerate((query_bias, None, value_bias)):
        at = pl.ds(part * D, D)
        made = mm(x_ref[...], weight[:, at])
        if bias is not None:
            made = made + vector(bias)
        qkv_ref[:, at] = made.astype(LOW)


def attend(qkv_ref, mask_ref, probs_ref, mixed_ref):
    first = lane_half(SEQ)

    @pl.loop(0, H // 2, unroll=True)
    def _(slab):
        queries = qkv_ref[:, columns(slab, SLAB)] * jnp.asarray(HD ** (-0.5), LOW)
        keys = qkv_ref[:, columns(slab + D // SLAB, SLAB)]
        values_t = qkv_ref[:, columns(slab + 2 * D // SLAB, SLAB)].T
        zero = jnp.zeros_like(keys)
        mixed = []
        for half in range(2):
            own = jnp.where(first, keys, zero) if half == 0 else jnp.where(first, zero, keys)
            scores = mm_nt(own, queries) + mask_ref[...]
            raised = jnp.exp(scores - jnp.max(scores, axis=0, keepdims=True))
            probs = (raised * (1.0 / jnp.sum(raised, axis=0, keepdims=True))).astype(LOW)
            if probs_ref is not None:
                probs_ref[2 * slab + half] = probs
            mixed.append(mm(values_t[half * HD : (half + 1) * HD], probs))
        mixed_ref[:, columns(slab, SLAB)] = jnp.concatenate(mixed, axis=0).T.astype(LOW)


def attend_back(qkv_ref, probs_ref, mixed_grad_ref, grad_ref):
    first = lane_half(SEQ)

    @pl.loop(0, H // 2, unroll=True)
    def _(slab):
        queries = qkv_ref[:, columns(slab, SLAB)] * jnp.asarray(HD ** (-0.5), LOW)
        keys_t = qkv_ref[:, columns(slab + D // SLAB, SLAB)].T
        values = qkv_ref[:, columns(slab + 2 * D // SLAB, SLAB)]
        grads = mixed_grad_ref[:, columns(slab, SLAB)]
        zero = jnp.zeros_like(values)
        query_grad, key_grad, value_grad = [], [], []
        for half in range(2):
            own = jnp.where(first, values, zero) if half == 0 else jnp.where(first, zero, values)
            probs = probs_ref[2 * slab + half]
            high = probs.astype(HIGH)
            product = high * mm_nt(own, grads)
            delta = jnp.sum(product, axis=0, keepdims=True)
            score_grad = (product - high * delta).astype(LOW)
            value_grad.append(mm(probs, grads))
            key_grad.append(mm(score_grad, queries))
            query_grad.append(mm(keys_t[half * HD : (half + 1) * HD], score_grad))
        grad_ref[:, columns(slab, SLAB)] = (
            jnp.concatenate(query_grad, axis=0).T * HD ** (-0.5)
        ).astype(LOW)
        grad_ref[:, columns(slab + D // SLAB, SLAB)] = jnp.where(first, *key_grad).astype(LOW)
        grad_ref[:, columns(slab + 2 * D // SLAB, SLAB)] = jnp.where(first, *value_grad).astype(LOW)


def first_norm(n, x, mixed):
    residual = x.astype(HIGH) + (mm(mixed, n.w_out[...]) + vector(n.out_bias))
    normed, inverse = normalize(residual)
    return normed, inverse, normed * vector(n.gain1) + vector(n.bias1)


def activate(n, low, act_ref, slope_ref):
    @pl.loop(0, FF // WIDE, unroll=True)
    def _(step):
        at = columns(step)
        before = mm(low, n.w_up[:, at]) + n.up_bias[:, at].astype(HIGH)
        share, bell = gelu_parts(before)
        act_ref[:, at] = (before * share).astype(LOW)
        if slope_ref is not None:
            slope_ref[:, at] = (share + before * bell * 0.3989422804014327).astype(LOW)


def second_norm(n, hidden, act):
    return normalize(hidden + (mm(act, n.w_down[...]) + vector(n.down_bias)))


def layer_out(n, normed):
    return (normed * vector(n.gain2) + vector(n.bias2)).astype(LOW)


def feed_back(n, copies, branch_grad, slope_ref, pre_grad_ref):
    for at in copies.by_blocks(n.place, n.w_down):
        act_grad = mm_nt(branch_grad, n.w_down[at, :])
        pre_grad_ref[:, at] = (act_grad * slope_ref[:, at].astype(HIGH)).astype(LOW)


def start_attention(place, x, pair_row, pair_col, vectors, pieces):
    rows = x.shape[0]
    k = Kernel(place)
    k.take(x=x, pair_row=pair_row, pair_col=pair_col)
    k.take(query_bias=vectors.query_bias, value_bias=vectors.value_bias)
    k.take_matrix(qkv=pieces.qkv)
    k.give(mixed=((rows, SEQ, D), LOW))
    k.hold(mask=((SEQ, SEQ), HIGH), qkv=STATE["qkv"])

    def body(n, copies):
        n.load(n.w_qkv)
        for row in range(rows):
            mask_into(n.pair_row.at[row], n.pair_col.at[row], n.mask)
            copies.ready(n.w_qkv)
            project(n.x.at[row], n.w_qkv, n.query_bias, n.value_bias, n.qkv)
            attend(n.qkv, n.mask, None, n.mixed.at[row])

    return k.run(body, 14).mixed


def start_middle(place, row, x, mixed, vectors, pieces):
    k = Kernel(place)
    k.pull_row(row, x=x, mixed=mixed)
    k.take(out_bias=vectors.out_bias, gain1=vectors.gain1)
    k.take(bias1=vectors.bias1, up_bias=vectors.up_bias)
    k.take_matrix(out=pieces.out, up=pieces.up)
    k.give(hidden=((SEQ, D), HIGH), act=((SEQ, FF), LOW))

    def body(n, copies):
        n.fetch(n.x, n.mixed)
        n.load(n.w_out, n.w_up)
        copies.ready(n.x, n.mixed, n.w_out)
        _, _, hidden = first_norm(n, n.x[...], n.mixed[...])
        n.hidden[...] = hidden
        copies.ready(n.w_up)
        activate(n, hidden.astype(LOW), n.act, None)

    outcome = k.run(body, 8)
    return outcome.hidden, outcome.act


def start_last(place, hidden, act, vectors, pieces):
    k = Kernel(place)
    k.pull(hidden=hidden, act=act)
    k.take(down_bias=vectors.down_bias, gain2=vectors.gain2, bias2=vectors.bias2)
    k.take_matrix(down=pieces.down)
    k.give(out=((SEQ, D), LOW))

    def body(n, copies):
        n.fetch(n.act, n.hidden)
        n.load(n.w_down)
        copies.ready(n.act, n.hidden)
        total = n.hidden[...] + vector(n.down_bias)
        for at in copies.by_blocks(n.place, n.w_down):
            total = total + mm(n.act[:, at], n.w_down[at, :])
        n.out[...] = layer_out(n, normalize(total)[0])

    return k.run(body, 6).out


def start_rest(place, row, x, mixed, vectors, pieces):
    k = Kernel(place)
    k.pull_row(row, x=x, mixed=mixed)
    k.take(out_bias=vectors.out_bias, gain1=vectors.gain1, bias1=vectors.bias1)
    k.take(up_bias=vectors.up_bias, down_bias=vectors.down_bias)
    k.take(gain2=vectors.gain2, bias2=vectors.bias2)
    k.take_matrix(out=pieces.out, up=pieces.up, down=pieces.down)
    k.give(out=((SEQ, D), LOW))
    k.hold(hidden=((SEQ, D), HIGH), act=((SEQ, FF), LOW))

    def body(n, copies):
        n.fetch(n.x, n.mixed)
        n.load(n.w_out, n.w_up, n.w_down)
        copies.ready(n.x, n.mixed, n.w_out)
        _, _, hidden = first_norm(n, n.x[...], n.mixed[...])
        n.hidden[...] = hidden
        copies.ready(n.w_up)
        activate(n, hidden.astype(LOW), n.act, None)
        copies.ready(n.w_down)
        n.out[...] = layer_out(n, second_norm(n, n.hidden[...], n.act[...])[0])

    return k.run(body, 10).out


def there_and_back(
    place, row, tokens, handed, gradient, pair_row, pair_col, vectors, pieces, before=None
):
    k = Kernel(place)
    k.pull_row(row, tokens=tokens, gradient=gradient)
    k.pull(handed=handed)
    k.take(pair_row=pair_row, pair_col=pair_col)
    k.take(**vars(vectors))
    k.take_matrix(**vars(pieces))
    k.give(out=((row + 1, SEQ, D), LOW), in_grad=((SEQ, D), LOW))
    if before is not None:
        k.take(before=before)
    k.give_far(**{"kept_" + name: like for name, like in STATE.items()})
    k.hold(**STATE)
    k.hold(
        resid=((SEQ, D), HIGH),
        pre_grad=((SEQ, FF), LOW),
        mixed_grad=((SEQ, D), LOW),
        proj_grad=((SEQ, 3 * D), LOW),
        mask=((SEQ, SEQ), HIGH),
    )

    def body(n, copies):
        def keep(**values):
            for name, value in values.items():
                if value is not None:
                    getattr(n, name)[...] = value
                copies.start(None, getattr(n, name), getattr(n, "kept_" + name))

        n.fetch(n.tokens, n.handed)
        n.load(n.w_qkv, n.w_out, n.w_up, n.w_down)
        n.fetch(n.gradient)
        copies.ready(n.tokens, n.handed)
        keep(x=jnp.where(n.place[2] == 0, n.tokens[...], n.handed[...]))
        mask_into(n.pair_row.at[row], n.pair_col.at[row], n.mask)
        copies.ready(n.w_qkv)
        project(n.x, n.w_qkv, n.query_bias, n.value_bias, n.qkv)
        keep(qkv=None)
        attend(n.qkv, n.mask, n.probs, n.mixed)
        keep(probs=None, mixed=None)
        copies.ready(n.w_out)
        normed, inverse, hidden = first_norm(n, n.x[...], n.mixed[...])
        n.resid[...] = hidden
        keep(normed1=normed, inverse1=inverse, low=hidden.astype(LOW))
        copies.ready(n.w_up)
        activate(n, n.low[...], n.act, n.slope)
        keep(act=None, slope=None)
        copies.ready(n.w_down)
        normed, inverse = second_norm(n, n.resid[...], n.act[...])
        keep(normed2=normed, inverse2=inverse)
        n.out[row] = layer_out(n, normed)
        if before is not None:
            n.out[:row] = n.before[...]

        copies.ready(n.gradient)
        resid = norm_back(
            n.gradient[...].astype(HIGH), n.normed2[...], n.inverse2[...], vector(n.gain2)
        )
        n.resid[...] = resid
        feed_back(n, copies, resid.astype(LOW), n.slope, n.pre_grad)
        hidden_grad = n.resid[...] + mm_nt(n.pre_grad[...], n.w_up[...])
        resid = norm_back(hidden_grad, n.normed1[...], n.inverse1[...], vector(n.gain1))
        n.resid[...] = resid
        n.mixed_grad[...] = mm_nt(resid.astype(LOW), n.w_out[...]).astype(LOW)
        attend_back(n.qkv, n.probs, n.mixed_grad, n.proj_grad)
        n.in_grad[...] = (n.resid[...] + mm_nt(n.proj_grad[...], n.w_qkv[...])).astype(LOW)

    outcome = k.run(body, 27)
    state = {name: getattr(outcome, "kept_" + name) for name in STATE}
    return outcome.out, outcome.in_grad, state


def take_rows(k, states, *names):
    for name in names:
        shape, kind = STATE[name]
        k.take_far(**{f"{name}_{row}": state[name] for row, state in enumerate(states)})
        k.hold(**{name: ((len(states) * shape[0], *shape[1:]), kind)})
        k.sems += len(states)


def fetch_rows(n, copies, **targets):
    for name, target in targets.items():
        length = STATE[name][0][0]
        for row in range(target.shape[0] // length):
            part = target.at[pl.ds(row * length, length)]
            copies.start(target, getattr(n, f"{name}_{row}"), part)


def parts_of(outcome):
    found = vars(outcome)
    return [(found["sent" + name[4:]], found[name]) for name in found if name[:4] == "kept"]


def send_blocks(n, copies):
    copies.blocks(n.place, n.stage, parts_of(n))


def product(stage, left, right):
    @pl.loop(0, stage.shape[1] // WIDE, unroll=True)
    def _(step):
        at = columns(step)
        stage[:, at] = mm_tn(left[...], right[:, at]).astype(LOW)


def pull_halves(k, **arrays):
    for name, value in arrays.items():
        k.take_far(**{"first_" + name: value})
        k.hold(**{name: ((2 * SEQ, *value.shape[1:]), value.dtype)})
        k.sems += 1


def fetch_halves(n, copies, **targets):
    for name, target in targets.items():
        copies.start(target, getattr(n, "first_" + name), target.at[pl.ds(0, SEQ)])


def add_sums(sums, at, **values):
    for value in values.values():
        put = slice(at, at + value.shape[1])
        sums[:, put] = sums[:, put] + value
        at += value.shape[1]


def feed_sums(sums, at, pre_grad, hidden_grad, normed, mixer_grad):
    add_sums(
        sums,
        at,
        up_bias=column_sum(pre_grad),
        gain1=column_sum(hidden_grad * normed),
        bias1=column_sum(hidden_grad),
        out_bias=column_sum(mixer_grad),
    )


def norm_sums(sums, gradient, normed, branch_grad):
    add_sums(
        sums,
        0,
        gain2=column_sum(gradient * normed),
        bias2=column_sum(gradient),
        down_bias=column_sum(branch_grad),
    )


def projection_sums(sums, proj_grad):
    add_sums(
        sums,
        SUMS_WIDTH - 2 * D,
        query_bias=column_sum(proj_grad[:, :D]),
        value_bias=column_sum(proj_grad[:, 2 * D :]),
    )


def back_first(place, cotangent, handed, state, vectors, pieces):
    k = Kernel(place)
    k.pull_row(0, cotangent=cotangent)
    k.pull(handed=handed)
    k.take(gain1=vectors.gain1, gain2=vectors.gain2)
    k.take_matrix(down=pieces.down, up=pieces.up)
    names = ("normed2", "inverse2", "slope", "normed1", "inverse1")
    k.pull(**{name: state[name] for name in names})
    k.put(
        branch_grad=((SEQ, D), LOW),
        pre_grad=((SEQ, FF), LOW),
        mixer_grad=((SEQ, D), LOW),
        resid=((SEQ, D), HIGH),
    )
    k.give(sums=((1, SUMS_WIDTH), HIGH))

    def body(n, copies):
        n.fetch(n.handed, n.cotangent, n.normed2, n.inverse2)
        n.fetch(n.slope)
        n.load(n.w_down)
        n.load(n.w_up)
        n.fetch(n.normed1, n.inverse1)
        n.sums[...] = jnp.zeros_like(n.sums)
        copies.ready(n.handed, n.cotangent, n.normed2, n.inverse2)
        gradient = jnp.where(n.place[2] == 0, n.handed[...], n.cotangent[...]).astype(HIGH)
        normed = n.normed2[...]
        resid = norm_back(gradient, normed, n.inverse2[...], vector(n.gain2))
        n.resid[...] = resid
        n.branch_grad[...] = resid.astype(LOW)
        n.send(n.branch_grad)
        norm_sums(n.sums, gradient, normed, n.branch_grad[...])
        copies.ready(n.slope)
        feed_back(n, copies, n.branch_grad[...], n.slope, n.pre_grad)
        n.send(n.pre_grad)
        copies.ready(n.w_up, n.normed1, n.inverse1)
        hidden_grad = n.resid[...] + mm_nt(n.pre_grad[...], n.w_up[...])
        normed = n.normed1[...]
        resid = norm_back(hidden_grad, normed, n.inverse1[...], vector(n.gain1))
        n.resid[...] = resid
        n.mixer_grad[...] = resid.astype(LOW)
        n.send(n.mixer_grad, n.resid)
        feed_sums(n.sums, 3 * D, n.pre_grad[...], hidden_grad, normed, n.mixer_grad[...])

    return k.run(body, 9)


def back_down(place, cotangent, handed, first, states, vectors):
    k = Kernel(place)
    k.pull_row(1, cotangent=cotangent)
    k.pull(handed=handed)
    k.take(gain2=vectors.gain2, first_sums=first.sums)
    k.pull(normed2=states[1]["normed2"], inverse2=states[1]["inverse2"])
    take_rows(k, states, "act")
    pull_halves(k, branch_grad=first.to_branch_grad)
    k.put(resid=((SEQ, D), HIGH))
    k.give_far(second_grad=((SEQ, D), LOW))
    k.give(sums=((1, SUMS_WIDTH), HIGH))
    half = FF // 8
    for part in range(2):
        k.give_far(**{f"sent{part}": ((half, 2 * D), LOW), f"kept{part}": ((half, 2 * D), LOW)})
        k.sems += 8
    k.hold(stage=((8 * half, D), LOW))

    def body(n, copies):
        n.fetch(n.handed, n.cotangent, n.normed2, n.inverse2)
        fetch_halves(n, copies, branch_grad=n.branch_grad)
        fetch_rows(n, copies, act=n.act)
        n.sums[...] = n.first_sums[...]
        copies.ready(n.handed, n.cotangent, n.normed2, n.inverse2)
        second = pl.ds(SEQ, SEQ)
        gradient = jnp.where(n.place[2] == 0, n.handed[...], n.cotangent[...]).astype(HIGH)
        normed = n.normed2[...]
        resid = norm_back(gradient, normed, n.inverse2[...], vector(n.gain2))
        n.resid[...] = resid
        n.branch_grad[second, :] = resid.astype(LOW)
        norm_sums(n.sums, gradient, normed, n.branch_grad[second, :])
        n.send(n.resid)
        copies.start(None, n.branch_grad.at[second, :], n.second_grad)
        copies.ready(n.act, n.branch_grad)
        for part, (sent, kept) in enumerate(parts_of(n)):
            for number in (1, 3, 0, 2):
                start = (n.place[0] ^ number) * (2 * half) + part * half
                at = pl.ds(pl.multiple_of(start, half), half)
                put = (4 * part + number) * half
                n.stage[pl.ds(put, half), :] = mm_tn(n.act[:, at], n.branch_grad[...]).astype(LOW)
                target, short = (kept, sent)[number % 2], half // 2
                for side in range(2):
                    into = target.at[pl.ds(number // 2 * short, short), pl.ds(side * D, D)]
                    copies.start(target, n.stage.at[pl.ds(put + side * short, short), :], into)

    outcome = k.run(body, 8)
    return outcome, parts_of(outcome)


def swap(value, axis, bit):
    devices = lax.axis_size(axis)
    return lax.ppermute(value, axis, [(i, i ^ bit) for i in range(devices)])


def half_of(shard):
    rows = shard.shape[0] // 2
    return lax.dynamic_slice_in_dim(shard, lax.axis_index("dp") % 2 * rows, rows, axis=0)


def all_pieces(shard, far, other):
    return [shard, far, other, swap(shard, "rep", 1), swap(far, "rep", 1), swap(other, "rep", 1)]


def add_low(*values):
    total = values[0].astype(HIGH)
    for value in values[1:]:
        total = total + value.astype(HIGH)
    return total.astype(LOW)


def after(value, *others):
    others = [other for other in others if other is not None]
    return lax.optimization_barrier((value, *others))[0] if others else value


def fit(value, shape):
    return jnp.pad(value, [(0, want - have) for want, have in zip(shape, value.shape)])


def common(first, second):
    return tuple(max(pair) for pair in zip(first.shape, second.shape))


class Reduction:
    def __init__(self):
        self.x, self.ends, self.across = [], [], []
        self.totals, self.finals = [], []
        self.waiting, self.payload = [], ()
        index = lax.axis_index("dp")
        self.line = lax.axis_size("dp") == 4
        self.edge = (index == 0) | (index == 3)

    def start(self, own, far, *deps):
        self.x.append(swap(after(far, *self.x[-1:], *deps), "rep", 2))
        total = add_low(*own, self.x[-1])
        if self.line:
            self.waiting.append(total)
        else:
            self.finals.append(lax.psum(total, "dp").astype(HIGH))

    def step(self, *deps):
        if self.line:
            self.turn(after(self.waiting.pop(0), *deps))

    def turn(self, total):
        at = len(self.ends)
        back = self.totals[at - BACK] if at >= BACK else None
        if total is None or back is None:
            payload = back if total is None else total
        else:
            shape = common(total, back)
            payload = jnp.where(self.edge, fit(total, shape), fit(back, shape))
        self.payload = (payload,)
        arrived = swap(after(payload, *self.ends[-1:]), "dp", 1)
        self.ends.append(arrived)
        if back is not None:
            here = arrived[: back.shape[0], : back.shape[1]]
            self.finals.append(jnp.where(self.edge, here, back).astype(HIGH))
        if total is not None:
            sums = add_low(total, arrived[: total.shape[0], : total.shape[1]])
            self.across.append(
                lax.ppermute(sums, "dp", [(1, 2), (2, 1)])
            )
            self.totals.append(add_low(sums, self.across[-1]))

    def finish(self):
        if self.line:
            for _ in range(BACK):
                self.turn(None)
        return self.finals


def between_cores(parts):
    own, far = [], []
    for sent, kept in parts:
        rows = kept.shape[0] // 2
        arrived = swap(sent, "rep", 1)
        own.append((kept[:rows], arrived[:rows]))
        far.append((kept[rows:], arrived[rows:]))
    return own, far


def spread(value):
    index = lax.axis_index("rep")
    for bit in (1, 2):
        other = swap(value, "rep", bit)
        high = (index & bit) > 0
        value = jnp.concatenate([jnp.where(high, other, value), jnp.where(high, value, other)])
    return value


def segment_ids(lengths):
    bounds = jnp.cumsum(lengths, axis=-1)
    places = jnp.arange(SEQ, dtype=jnp.int32)
    return jnp.sum((places[None, :, None] >= bounds[:, None, :]).astype(jnp.int32), axis=-1)


def per_device(
    tokens,
    cotangent,
    pair_lengths,
    qkv_weight,
    out_weight,
    up_weight,
    down_weight,
    query_bias,
    value_bias,
    out_bias,
    norm1_gain,
    norm1_bias,
    up_bias,
    down_bias,
    norm2_gain,
    norm2_bias,
):
    rows = tokens.shape[0]
    place = jnp.stack(
        [lax.axis_index("rep"), lax.axis_index("dp") % 2, lax.axis_index("section")]
    ).astype(jnp.int32)
    vectors = SimpleNamespace(
        query_bias=query_bias,
        value_bias=value_bias,
        out_bias=out_bias,
        gain1=norm1_gain,
        bias1=norm1_bias,
        up_bias=up_bias,
        down_bias=down_bias,
        gain2=norm2_gain,
        bias2=norm2_bias,
    )
    pairs = segment_ids(pair_lengths)
    pair_row, pair_col = pairs[:, None, :], pairs[:, :, None]

    shards = SimpleNamespace(
        qkv=qkv_weight[0],
        mid=jnp.concatenate([out_weight[0], up_weight[0]], axis=1),
        down=down_weight[0],
    )
    far, other, pieces = SimpleNamespace(), SimpleNamespace(), SimpleNamespace()
    far.qkv = swap(half_of(shards.qkv), "rep", 2)
    other.qkv = swap(far.qkv, "dp", 1)
    pieces.qkv = all_pieces(shards.qkv, far.qkv, other.qkv)
    far.mid = swap(after(half_of(shards.mid), far.qkv), "rep", 2)
    mixed = start_attention(after(place, far.mid), tokens, pair_row, pair_col, vectors, pieces)
    other.mid = swap(far.mid, "dp", 1)
    far.down = swap(after(half_of(shards.down), far.mid), "rep", 2)
    pieces.up = all_pieces(shards.mid, far.mid, after(other.mid, mixed, far.down))
    pieces.out = pieces.up
    other.down = swap(after(far.down, other.mid, mixed), "dp", 1)
    hidden, act = start_middle(place, 0, tokens, mixed, vectors, pieces)
    pieces.down = all_pieces(shards.down, far.down, after(other.down, act))
    out = start_last(place, hidden, act, vectors, pieces)
    handed = [lax.ppermute(out, "section", [(0, 1)])]
    out = start_rest(after(place, out), 1, tokens, mixed, vectors, pieces)
    handed.append(lax.ppermute(out, "section", [(0, 1)]))

    out, states, handed_back = None, [], []
    for row in range(rows):
        out, in_grad, state = there_and_back(
            place, row, tokens, handed[row], cotangent, pair_row, pair_col, vectors, pieces, out
        )
        states.append(state)
        handed_back.append(lax.ppermute(in_grad, "section", [(1, 0)]))

    reduction = Reduction()
    first = back_first(place, cotangent, handed_back[0], states[0], vectors, pieces)
    fed, down_parts = back_down(place, cotangent, handed_back[1], first, states, vectors)
    own, far = between_cores(down_parts)
    fars = [add_low(*item) for item in far]
    hid = back_up(
        after(place, fars[0], fars[1]),
        fed.second_grad,
        fed.to_resid,
        fed.sums,
        first,
        states,
        vectors,
        pieces,
    )
    reduction.start(own[0], fars[0])
    sent_up = after(hid.sent_up, reduction.x[0])
    up_own, up_far = between_cores([(sent_up, hid.kept_up)])
    out_own, out_far = between_cores([(hid.sent_out, hid.kept_out)])
    reduction.start(own[1], fars[1])
    reduction.step()
    mix = back_mix(
        after(place, reduction.x[0]),
        (first.to_mixer_grad, hid.second_grad),
        (first.to_resid, hid.to_resid),
        hid.sums,
        states,
        pieces,
    )
    sent = after(mix.sent0, reduction.x[1], *reduction.ends[:1])
    own, far = between_cores([(sent, mix.kept0)])

    def beside(left, right):
        left = [jnp.pad(value, [(0, EXTRA), (0, 0)]) for value in left]
        return [jnp.concatenate([a, b[:, :D]], axis=1) for a, b in zip(left, right)]

    half = FF // 2
    reduction.start([v[:, :half] for v in up_own[0]], add_low(*[v[:, :half] for v in up_far[0]]))
    reduction.step()
    reduction.step(reduction.x[2])
    reduction.start(
        [v[:, half:] for v in up_own[0]], add_low(*[v[:, half:] for v in up_far[0]]), *reduction.payload
    )
    reduction.step(reduction.x[3])
    reduction.start(
        beside(out_own[0], own[0]), add_low(*beside(out_far[0], far[0])), *reduction.payload
    )
    reduction.step(reduction.x[4])
    tail = [[v[: D // 4, D:] for v in values] for values in (own[0], far[0])]
    reduction.start(tail[0], add_low(*tail[1]), *reduction.payload)
    reduction.step()
    down0, down1, up0, up1, beside, qkv = reduction.finish()
    block = beside[D // 4 :, D:]
    sums = spread(block[:3].reshape(3 * D).astype(LOW))[None].astype(HIGH)
    totals = [
        jnp.concatenate([beside[: D // 4, D:], qkv], axis=1),
        beside[: D // 4, :D],
        jnp.concatenate([up0, up1], axis=1),
        jnp.concatenate([down0[:, :D], down0[:, D:], down1[:, :D], down1[:, D:]], axis=0),
    ]
    vector_totals = [
        sums[:, SUM_AT[name][0] : SUM_AT[name][0] + SUM_AT[name][1]] for name in vars(vectors)
    ]
    return (
        out[None],
        mix.in_grad[None],
        *[total[None] for total in totals],
        *vector_totals,
    )


def solution(mesh):
    rows = P(("dp", "rep"), None, None)
    matrix = P("section", "rep", None)
    row = P("section", None)
    made = P("section", ("dp", "rep"), None, None)
    return jax.shard_map(
        per_device,
        mesh=mesh,
        in_specs=(rows, rows, P(("dp", "rep"), None)) + (matrix,) * 4 + (row,) * 9,
        out_specs=(made, made) + (matrix,) * 4 + (row,) * 9,
        check_vma=False,
    )
```
